256 devices in a mesh: island: 16 (over y_hi, x, core), fsdp: 16 (over y_lo, z).
Axes of the slice: x: 4, y: 4 (y_hi: 2, y_lo: 2; y = y_hi * 2 + y_lo), z: 8, core: 2. Of those that a mesh axis runs over, the one named last changes fastest.
Arguments:
- inputs: bfloat16 [16, 4096, 8192], P('island', 'fsdp'), may hold values from -6 to 6
- cotangent: bfloat16 [16, 4096, 512], P('island', 'fsdp'), may hold values from -6 to 6
- key_weight: bfloat16 [16, 8192, 512], P('island', 'fsdp'), may hold values from -0.0625 to 0.0625
- pseudo_grads: bfloat16 [16, 8192, 512], P('island', 'fsdp'), may hold values from -3 to 3
- outer_params: float32 [8192, 512], P('fsdp'), may hold values from -6 to 6
- outer_momentum: float32 [8192, 512], P('fsdp'), may hold values from -3 to 3
Outputs:
- input_grads: bfloat16 [16, 4096, 8192], P('island', 'fsdp')
- weight_grads: float32 [16, 8192, 512], P('island', 'fsdp')
- new_params: float32 [8192, 512], P('fsdp')
- new_momentum: float32 [8192, 512], P('fsdp')
The draws below stay inside these ranges and needn't reach their ends.
All inputs are finite; a program needn't handle non-finite values.
Results may differ from the reference program's by a relative error of at most 0.0055.
Values may be sent and summed in bfloat16 or wider, within the bound.
A program may use at most 128 MiB of HBM per device.

```python
import jax
import jax.numpy as jnp
from jax import lax

D = 8192
OUTER_W = 512
KW = 512
TOKENS = 4096
ISLANDS = 16


def spiked(values, rng, source, target, blocks, factor):
    def block_of(dim):
        return (jnp.arange(values.shape[dim]) // (values.shape[dim] // blocks)).reshape((-1,) + (1,) * (values.ndim - 1 - dim))

    first = jax.random.permutation(rng, blocks)[block_of(target)]
    far = (block_of(target) + blocks // 2) % blocks
    return jnp.where((block_of(source) == first) | (block_of(source) == far), factor * values, values)


def shard_levels(key, shape, pieces, smallest, high):
    def one(dim, shards_of):
        heights = jax.random.uniform(jax.random.fold_in(jax.random.fold_in(key, 6), dim), (shards_of,), jnp.float32, smallest / len(pieces), high / len(pieces))
        return jnp.repeat(jnp.exp(heights), shape[dim] // shards_of).reshape((-1,) + (1,) * (len(shape) - dim - 1))

    gain = one(*pieces[0])
    for cut in pieces[1:]:
        gain = gain * one(*cut)
    return gain


def centred(own_key, dims, deviation, bound, cuts=(), held_as=jnp.bfloat16):
    values = deviation * jax.random.normal(own_key, dims, jnp.float32)
    if cuts:
        values = values * shard_levels(own_key, dims, cuts, -0.22, 0.18)
    return jnp.clip(values, -bound, bound).astype(held_as)


def heavy_noise(own_key, extent, width, reach, pieces, heavy, kind=jnp.bfloat16):
    result = width * jax.random.normal(own_key, extent, jnp.float32)
    if pieces:
        result = result * shard_levels(own_key, extent, pieces, -0.22, 0.18)
    return jnp.clip(spiked(result, jax.random.fold_in(own_key, 3), *heavy), -reach, reach).astype(kind)


def setup_inputs(seed: int = 0) -> dict:
    keys = jax.random.split(jax.random.key(seed), 7)
    return {
        "inputs": heavy_noise(keys[0], (ISLANDS, TOKENS, D), 1.0, 6.0, ((0, 16), (1, 16)), (1, 2, 16, 2.0)),
        "cotangent": centred(keys[1], (ISLANDS, TOKENS, KW), 1.0, 6.0, ((0, 16), (1, 16))),
        "key_weight": centred(keys[2], (ISLANDS, D, KW), D ** -0.5, 0.0625, ((0, 16), (1, 16))),
        "pseudo_grads": centred(keys[3], (ISLANDS, D, OUTER_W), 0.5, 3.0, ((0, 16), (1, 16))),
        "outer_params": centred(keys[4], (D, OUTER_W), 1.0, 6.0, ((0, 16),), jnp.float32),
        "outer_momentum": centred(keys[5], (D, OUTER_W), 0.5, 3.0, ((0, 16),), jnp.float32),
    }


outer_rate = 0.7
outer_beta = 0.9


def island_grads(island_args):
    features, cot_rows, weight_rows = island_args
    input_grad = lax.dot_general(cot_rows, weight_rows, (((1,), (1,)), ((), ())), preferred_element_type=jnp.float32).astype(jnp.bfloat16)
    weight_grad = lax.dot_general(features, cot_rows, (((0,), (0,)), ((), ())), preferred_element_type=jnp.float32) / TOKENS
    return input_grad, weight_grad


def reference(inputs, cotangent, key_weight, pseudo_grads, outer_params, outer_momentum):
    input_grads, weight_grads = lax.map(island_grads, (inputs, cotangent, key_weight))
    average = jnp.sum(pseudo_grads.astype(jnp.float32), axis=0) / ISLANDS
    new_momentum = outer_beta * outer_momentum + average
    new_params = outer_params - outer_rate * (average + outer_beta * new_momentum)
    return input_grads, weight_grads, new_params, new_momentum
```

```python
import functools

import jax
import jax.numpy as jnp
from jax import lax
from jax.experimental import pallas as pl
from jax.experimental.pallas import tpu as pltpu
from jax.sharding import PartitionSpec as P

outer_rate = 0.7
outer_beta = 0.9

MESH = pl.DeviceIdType.MESH
F32 = jnp.float32
BF16 = jnp.bfloat16

Z = 8
PLANE = 8
ROWS = 512
HALF = ROWS // 2
TOK = 256
PURE = 128
HYB = ROWS - PURE
KW = 512
PIECE = ROWS // PLANE

UP, DOWN = 0, 1


def rows(start, size):
    return pl.ds(start, size)


def kernel(
    x_ref, c_ref, w_ref, pg_ref, op_ref, om_ref,
    ig_ref, wg_ref, np_ref, nm_ref,
    cot, xin, wb, term, rs_in, rs_out, ig_far, ig_own, ig_pure,
    pg_own, c_in, c_out, c_far, avg, opb, omb, npb, nmb, wgb,
    ag_s, ag_r, rs_s, rs_r, yx_s, yx_r, yc_s, yc_r, yw_s, yw_r, yi_s, yi_r,
    c1_s, c1_r, c2_s, c2_r, c3_s, c3_r, lx, lm, lo, lw,
):
    isl = lax.axis_index("island")
    fs = lax.axis_index("fsdp")
    z, yl = lax.rem(fs, Z), fs // Z
    q, yh = lax.rem(isl, PLANE), isl // PLANE
    up = (isl, yl * Z + lax.rem(z + 1, Z))
    down = (isl, yl * Z + lax.rem(z + Z - 1, Z))
    pair = (isl, (1 - yl) * Z + z)
    far = ((1 - yh) * PLANE + q, fs)
    plane = [(yh * PLANE + lax.rem(q + j, PLANE), fs) for j in range(1, PLANE)]
    ring = (up, down)

    barrier = pltpu.get_barrier_semaphore()
    for peer in [up, down, pair, far] + plane:
        pl.semaphore_signal(barrier, inc=1, device_id=peer, device_id_type=MESH)

    def remote(src, dst, ss, rs, peer):
        return pltpu.make_async_remote_copy(
            src_ref=src, dst_ref=dst, send_sem=ss, recv_sem=rs, device_id=peer, device_id_type=MESH
        )

    def columns(owner_yl, s):
        return pl.ds(pl.multiple_of((owner_yl * Z + lax.rem(z + s, Z)) * ROWS, ROWS), ROWS)

    local = [
        pltpu.make_async_copy(c_ref.at[0], cot.at[rows(0, TOK)], lm.at[0]),
        pltpu.make_async_copy(w_ref.at[0], wb.at[0, rows(0, ROWS)], lm.at[1]),
        pltpu.make_async_copy(
            pg_ref.at[0, pl.ds(pl.multiple_of(q * PIECE, PIECE), PIECE)], pg_own, lm.at[2]
        ),
        pltpu.make_async_copy(op_ref, opb, lm.at[3]),
        pltpu.make_async_copy(om_ref, omb, lm.at[4]),
    ]
    own_x = [
        pltpu.make_async_copy(x_ref.at[0, :, columns(yl, s)], xin.at[s, rows(0, TOK)], lx.at[s])
        for s in range(Z)
    ]
    for copy in local:
        copy.start()
    for s in (4, 3, 5, 2, 6, 1, 7, 0):
        own_x[s].start()

    y_w = remote(w_ref.at[0, rows(0, PURE)], wb.at[0, rows(ROWS, PURE)], yw_s, yw_r, pair)
    y_c = remote(c_ref.at[0], cot.at[rows(TOK, TOK)], yc_s, yc_r, pair)
    y_x = [
        remote(x_ref.at[0, :, columns(1 - yl, s)], xin.at[s, rows(TOK, TOK)], yx_s.at[s], yx_r.at[s], pair)
        for s in range(Z)
    ]

    cuts = {
        0: (0, HALF),
        1: (HALF, HALF),
        2: (ROWS, PURE),
        3: (ROWS, PURE // 2),
        4: (ROWS + PURE // 2, PURE // 2),
    }

    def slot(d, r):
        return r if d == UP else (Z - r) % Z

    def gather(d, r, c):
        start, size = cuts[c]
        src = w_ref.at[0, rows(start, size)] if r == 0 and c < 2 else wb.at[slot(d, r), rows(start, size)]
        dst = wb.at[slot(d, r + 1), rows(start, size)]
        n = min(c, 2)
        return remote(src, dst, ag_s.at[d, r, n], ag_r.at[d, r, n], ring[d])

    first = {UP: 0, DOWN: 1}
    last_pure = {UP: 3, DOWN: 4}

    c_1 = [
        remote(
            pg_ref.at[0, pl.ds(pl.multiple_of(lax.rem(q + j, PLANE) * PIECE, PIECE), PIECE)],
            c_in.at[j - 1], c1_s.at[j - 1], c1_r.at[j - 1], plane[j - 1],
        )
        for j in range(1, PLANE)
    ]
    c_2 = remote(c_out, c_far, c2_s, c2_r, far)
    own_piece = pl.ds(pl.multiple_of(q * PIECE, PIECE), PIECE)
    c_3 = [
        remote(avg.at[own_piece], avg.at[own_piece], c3_s.at[j - 1], c3_r.at[j - 1], plane[j - 1])
        for j in range(1, PLANE)
    ]

    def c_3_arrival(j):
        piece = pl.ds(pl.multiple_of(lax.rem(q + PLANE - j, PLANE) * PIECE, PIECE), PIECE)
        return remote(avg.at[piece], avg.at[piece], c3_s.at[j - 1], c3_r.at[j - 1], plane[j - 1])

    half_of = {UP: (0, 1), DOWN: (1, 0)}

    def reduce_copy(d, k, h):
        part = rows(h * HALF, HALF)
        return remote(
            rs_out.at[d, k - 1, part], rs_in.at[d, k - 1, part],
            rs_s.at[d, k - 1, h], rs_r.at[d, k - 1, h], ring[d],
        )

    def target(d, k):
        return k if d == UP else Z - k

    def send_sum(d, k, h, chained):
        part = rows(h * HALF, HALF)
        total = term[target(d, k), part, :]
        if chained:
            reduce_copy(d, k + 1, h).wait_recv()
            total = total + rs_in[d, k, part, :].astype(F32)
        rs_out[d, k - 1, part, :] = total.astype(BF16)
        reduce_copy(d, k, h).start()

    def make_term(s):
        own_x[s].wait()
        y_x[s].wait_recv()

        @pl.loop(0, ROWS // 256)
        def _(i):
            part = pl.ds(pl.multiple_of(i * 256, 256), 256)
            term[s, part, :] = lax.dot_general(
                xin[s, :, part], cot[...], (((0,), (0,)), ((), ())), preferred_element_type=F32
            )

    out_copies = []

    def ig_copy(r):
        cols = columns(yl, Z - r)
        mine = pltpu.make_async_copy(ig_own.at[r], ig_ref.at[0, :, cols], lo.at[0, r])
        start = pl.multiple_of(((1 - yl) * Z + lax.rem(z + Z - r, Z)) * ROWS, ROWS)
        pure = pltpu.make_async_copy(ig_pure.at[r], ig_ref.at[0, :, pl.ds(start, PURE)], lo.at[1, r])
        start = pl.multiple_of((yl * Z + lax.rem(z + Z - r, Z)) * ROWS + PURE, 128)
        sent = remote(
            ig_far.at[r], ig_ref.at[0, :, pl.ds(start, HYB)], yi_s.at[r], yi_r.at[r], pair
        )
        return mine, pure, sent

    def make_ig(r):
        transposed = (((1,), (1,)), ((), ()))
        ig_far[r] = lax.dot_general(
            cot[TOK:, :], wb[r, PURE:ROWS, :], transposed, preferred_element_type=F32
        ).astype(BF16)
        mine, pure, sent = ig_copy(r)
        sent.start()
        ig_own[r] = lax.dot_general(
            cot[:TOK, :], wb[r, :ROWS, :], transposed, preferred_element_type=F32
        ).astype(BF16)
        mine.start()
        ig_pure[r] = lax.dot_general(
            cot[:TOK, :], wb[r, ROWS:, :], transposed, preferred_element_type=F32
        ).astype(BF16)
        pure.start()

    def pass_on(r, i):
        for d in (UP, DOWN):
            c = 2 if i == 2 else (first[d] if i == 0 else 1 - first[d])
            gather(d, r, c).wait_recv()
            if r + 1 < 3:
                gather(d, r + 1, c).start()
            elif r + 1 == 3 and i == 0:
                gather(d, 3, c).start()
            elif r + 1 == 3 and i == 2:
                gather(d, 3, last_pure[d]).start()

    pl.semaphore_wait(barrier, 4 + len(plane))

    y_w.start()
    for d in (UP, DOWN):
        gather(d, 0, first[d]).start()
        gather(d, 0, 1 - first[d]).start()
    y_c.start()
    for s in (4, 3, 5, 2):
        y_x[s].start()
    for copy in c_1:
        copy.start()

    y_w.wait_recv()
    for d in (UP, DOWN):
        gather(d, 0, 2).start()
    pass_on(0, 0)
    for copy in local[:3]:
        copy.wait()
    total = pg_own[...].astype(F32)
    for j in range(1, PLANE):
        c_1[j - 1].wait_recv()
        total = total + c_in[j - 1].astype(F32)
    c_out[...] = total.astype(BF16)
    c_2.start()
    for s in (6, 1, 7, 0):
        y_x[s].start()
    y_c.wait_recv()
    make_ig(0)
    pass_on(0, 1)
    pass_on(0, 2)
    make_term(4)
    make_ig(1)
    make_ig(7)
    pass_on(1, 0)
    make_term(3)
    pass_on(1, 1)
    make_term(5)
    pass_on(1, 2)
    make_ig(2)
    make_ig(6)
    make_term(2)
    pass_on(2, 0)
    c_2.wait_recv()
    avg[own_piece, :] = (c_out[...].astype(F32) + c_far[...].astype(F32)) * (1.0 / 16)
    for copy in c_3:
        copy.start()
    make_term(6)
    pass_on(2, 1)
    pass_on(2, 2)
    for d in (UP, DOWN):
        send_sum(d, 4, half_of[d][0], False)
    for d in (UP, DOWN):
        send_sum(d, 3, half_of[d][1], False)
    make_ig(3)
    make_ig(5)
    make_term(1)
    for d in (UP, DOWN):
        gather(d, 3, first[d]).wait_recv()
        gather(d, 3, last_pure[d]).wait_recv()
    make_ig(4)
    make_term(7)
    for d in (UP, DOWN):
        send_sum(d, 3, half_of[d][0], True)
    make_term(0)
    for h in (1, 0):
        for d in (UP, DOWN):
            send_sum(d, 2, half_of[d][h], True)

    for copy in local[3:]:
        copy.wait()
    for j in range(1, PLANE):
        c_3_arrival(j).wait_recv()

    @pl.loop(0, ROWS // 64)
    def _(i):
        part = pl.ds(pl.multiple_of(i * 64, 64), 64)
        average = avg[part, :]
        momentum = outer_beta * omb[part, :] + average
        nmb[part, :] = momentum
        npb[part, :] = opb[part, :] - outer_rate * (average + outer_beta * momentum)

    outer = [
        pltpu.make_async_copy(npb, np_ref, lm.at[5]),
        pltpu.make_async_copy(nmb, nm_ref, lm.at[6]),
    ]
    for copy in outer:
        copy.start()

    for h in (1, 0):
        for d in (UP, DOWN):
            send_sum(d, 1, half_of[d][h], True)
    for d in (UP, DOWN):
        for h in (1, 0):
            reduce_copy(d, 1, half_of[d][h]).wait_recv()
    wg_copies = []
    for h in (0, 1):
        part = rows(h * HALF, HALF)
        wgb[part, :] = (
            term[0, part, :] + rs_in[UP, 0, part, :].astype(F32) + rs_in[DOWN, 0, part, :].astype(F32)
        ) * (1.0 / 4096)
        copy = pltpu.make_async_copy(wgb.at[part], wg_ref.at[0, part], lw.at[h])
        copy.start()
        wg_copies.append(copy)

    for r in range(Z):
        mine, pure, sent = ig_copy(r)
        mine.wait()
        pure.wait()
        sent.wait_send()
    for copy in outer + wg_copies:
        copy.wait()
    y_w.wait_send()
    y_c.wait_send()
    c_2.wait_send()
    for s in range(Z):
        y_x[s].wait_send()
    for j in range(1, PLANE):
        c_1[j - 1].wait_send()
        c_3[j - 1].wait_send()
    for d in (UP, DOWN):
        for r in range(3):
            for c in range(3):
                gather(d, r, c).wait_send()
        gather(d, 3, first[d]).wait_send()
        gather(d, 3, last_pure[d]).wait_send()
        reduce_copy(d, 4, half_of[d][0]).wait_send()
        for k in (3, 2, 1):
            for h in (0, 1):
                reduce_copy(d, k, h).wait_send()
    for r in range(Z):
        start = pl.multiple_of(((1 - yl) * Z + lax.rem(z + Z - r, Z)) * ROWS + PURE, 128)
        remote(
            ig_far.at[r], ig_ref.at[0, :, pl.ds(start, HYB)], yi_s.at[r], yi_r.at[r], pair
        ).wait_recv()


def body(inputs, cotangent, key_weight, pseudo_grads, outer_params, outer_momentum):
    dma = pltpu.SemaphoreType.DMA
    vmem = pltpu.VMEM
    anywhere = pl.BlockSpec(memory_space=pl.ANY)
    return pl.pallas_call(
        kernel,
        name="key_backward",
        out_shape=(
            jax.ShapeDtypeStruct((1, TOK, 2 * Z * ROWS), BF16),
            jax.ShapeDtypeStruct((1, ROWS, KW), F32),
            jax.ShapeDtypeStruct((ROWS, KW), F32),
            jax.ShapeDtypeStruct((ROWS, KW), F32),
        ),
        in_specs=[anywhere] * 6,
        out_specs=(anywhere,) * 4,
        scratch_shapes=[
            vmem((2 * TOK, KW), BF16),
            vmem((Z, 2 * TOK, ROWS), BF16),
            vmem((Z, ROWS + PURE, KW), BF16),
            vmem((Z, ROWS, KW), F32),
            vmem((2, 4, ROWS, KW), BF16),
            vmem((2, 4, ROWS, KW), BF16),
            vmem((Z, TOK, HYB), BF16),
            vmem((Z, TOK, ROWS), BF16),
            vmem((Z, TOK, PURE), BF16),
            vmem((PIECE, KW), BF16),
            vmem((PLANE - 1, PIECE, KW), BF16),
            vmem((PIECE, KW), BF16),
            vmem((PIECE, KW), BF16),
            vmem((ROWS, KW), F32),
            vmem((ROWS, KW), F32),
            vmem((ROWS, KW), F32),
            vmem((ROWS, KW), F32),
            vmem((ROWS, KW), F32),
            vmem((ROWS, KW), F32),
            dma((2, 4, 3)), dma((2, 4, 3)),
            dma((2, 4, 2)), dma((2, 4, 2)),
            dma((Z,)), dma((Z,)),
            dma, dma, dma, dma,
            dma((Z,)), dma((Z,)),
            dma((PLANE - 1,)), dma((PLANE - 1,)),
            dma, dma,
            dma((PLANE - 1,)), dma((PLANE - 1,)),
            dma((Z,)), dma((7,)), dma((2, Z)), dma((2,)),
        ],
        compiler_params=pltpu.CompilerParams(
            collective_id=0, has_side_effects=True, vmem_limit_bytes=56 * 2**20
        ),
        cost_estimate=pl.CostEstimate(
            flops=4 * TOK * 2 * Z * ROWS * KW, bytes_accessed=24 * 2**20, transcendentals=0
        ),
    )(inputs, cotangent, key_weight, pseudo_grads, outer_params, outer_momentum)


def solution(mesh):
    return jax.shard_map(
        body,
        mesh=mesh,
        in_specs=(
            P("island", "fsdp", None),
            P("island", "fsdp", None),
            P("island", "fsdp", None),
            P("island", "fsdp", None),
            P("fsdp", None),
            P("fsdp", None),
        ),
        out_specs=(
            P("island", "fsdp", None),
            P("island", "fsdp", None),
            P("fsdp", None),
            P("fsdp", None),
        ),
        check_vma=False,
    )
```

```python
import functools

import jax
import jax.numpy as jnp
from jax import lax
from jax.experimental import pallas as pl
from jax.experimental.pallas import tpu as pltpu
from jax.sharding import PartitionSpec as P

outer_rate = 0.7
outer_beta = 0.9

MESH = pl.DeviceIdType.MESH
F32 = jnp.float32
BF16 = jnp.bfloat16

Z = 8
PLANE = 8
ROWS = 512
HALF = ROWS // 2
TOK = 256
PURE = 128
HYB = ROWS - PURE
KW = 512
PIECE = ROWS // PLANE

UP, DOWN = 0, 1


def rows(start, size):
    return pl.ds(start, size)


def kernel(
    x_ref, c_ref, w_ref, pg_ref, op_ref, om_ref,
    ig_ref, wg_ref, np_ref, nm_ref,
    cot, xin, wb, term, rs_in, rs_out, ig_far,
    pg_own, c_in, c_out, c_far, avg, opb, omb,
    ag_s, ag_r, rs_s, rs_r, yx_s, yx_r, yc_s, yc_r, yw_s, yw_r, yi_s, yi_r,
    c1_s, c1_r, c2_s, c2_r, c3_s, c3_r, lx, lm,
):
    isl = lax.axis_index("island")
    fs = lax.axis_index("fsdp")
    z, yl = lax.rem(fs, Z), fs // Z
    q, yh = lax.rem(isl, PLANE), isl // PLANE
    up = (isl, yl * Z + lax.rem(z + 1, Z))
    down = (isl, yl * Z + lax.rem(z + Z - 1, Z))
    pair = (isl, (1 - yl) * Z + z)
    far = ((1 - yh) * PLANE + q, fs)
    plane = [(yh * PLANE + lax.rem(q + j, PLANE), fs) for j in range(1, PLANE)]
    ring = (up, down)

    barrier = pltpu.get_barrier_semaphore()
    for peer in [up, down, pair, far] + plane:
        pl.semaphore_signal(barrier, inc=1, device_id=peer, device_id_type=MESH)

    def remote(src, dst, ss, rs, peer):
        return pltpu.make_async_remote_copy(
            src_ref=src, dst_ref=dst, send_sem=ss, recv_sem=rs, device_id=peer, device_id_type=MESH
        )

    def columns(owner_yl, s):
        return pl.ds(pl.multiple_of((owner_yl * Z + lax.rem(z + s, Z)) * ROWS, ROWS), ROWS)

    local = [
        pltpu.make_async_copy(c_ref.at[0], cot.at[rows(0, TOK)], lm.at[0]),
        pltpu.make_async_copy(w_ref.at[0], wb.at[0, rows(0, ROWS)], lm.at[1]),
        pltpu.make_async_copy(
            pg_ref.at[0, pl.ds(pl.multiple_of(q * PIECE, PIECE), PIECE)], pg_own, lm.at[2]
        ),
        pltpu.make_async_copy(op_ref, opb, lm.at[3]),
        pltpu.make_async_copy(om_ref, omb, lm.at[4]),
    ]
    own_x = [
        pltpu.make_async_copy(x_ref.at[0, :, columns(yl, s)], xin.at[s, rows(0, TOK)], lx.at[s])
        for s in range(Z)
    ]
    for copy in local:
        copy.start()
    for s in (4, 3, 5, 2, 6, 1, 7, 0):
        own_x[s].start()

    y_w = remote(w_ref.at[0, rows(0, PURE)], wb.at[0, rows(ROWS, PURE)], yw_s, yw_r, pair)
    y_c = remote(c_ref.at[0], cot.at[rows(TOK, TOK)], yc_s, yc_r, pair)
    y_x = [
        remote(x_ref.at[0, :, columns(1 - yl, s)], xin.at[s, rows(TOK, TOK)], yx_s.at[s], yx_r.at[s], pair)
        for s in range(Z)
    ]

    cuts = {
        0: (0, HALF),
        1: (HALF, HALF),
        2: (ROWS, PURE),
        3: (ROWS, PURE // 2),
        4: (ROWS + PURE // 2, PURE // 2),
    }

    def slot(d, r):
        return r if d == UP else (Z - r) % Z

    def gather(d, r, c):
        start, size = cuts[c]
        src = w_ref.at[0, rows(start, size)] if r == 0 and c < 2 else wb.at[slot(d, r), rows(start, size)]
        dst = wb.at[slot(d, r + 1), rows(start, size)]
        n = min(c, 2)
        return remote(src, dst, ag_s.at[d, r, n], ag_r.at[d, r, n], ring[d])

    first = {UP: 0, DOWN: 1}
    last_pure = {UP: 3, DOWN: 4}

    c_1 = [
        remote(
            pg_ref.at[0, pl.ds(pl.multiple_of(lax.rem(q + j, PLANE) * PIECE, PIECE), PIECE)],
            c_in.at[j - 1], c1_s.at[j - 1], c1_r.at[j - 1], plane[j - 1],
        )
        for j in range(1, PLANE)
    ]
    c_2 = remote(c_out, c_far, c2_s, c2_r, far)
    own_piece = pl.ds(pl.multiple_of(q * PIECE, PIECE), PIECE)
    c_3 = [
        remote(avg.at[own_piece], avg.at[own_piece], c3_s.at[j - 1], c3_r.at[j - 1], plane[j - 1])
        for j in range(1, PLANE)
    ]

    def c_3_arrival(j):
        piece = pl.ds(pl.multiple_of(lax.rem(q + PLANE - j, PLANE) * PIECE, PIECE), PIECE)
        return remote(avg.at[piece], avg.at[piece], c3_s.at[j - 1], c3_r.at[j - 1], plane[j - 1])

    half_of = {UP: (0, 1), DOWN: (1, 0)}

    def reduce_copy(d, k, h):
        part = rows(h * HALF, HALF)
        return remote(
            rs_out.at[d, k - 1, part], rs_in.at[d, k - 1, part],
            rs_s.at[d, k - 1, h], rs_r.at[d, k - 1, h], ring[d],
        )

    def target(d, k):
        return k if d == UP else Z - k

    def send_sum(d, k, h, chained):
        part = rows(h * HALF, HALF)
        total = term[target(d, k), part, :]
        if chained:
            reduce_copy(d, k + 1, h).wait_recv()
            total = total + rs_in[d, k, part, :].astype(F32)
        rs_out[d, k - 1, part, :] = total.astype(BF16)
        reduce_copy(d, k, h).start()

    def make_term(s):
        own_x[s].wait()
        y_x[s].wait_recv()

        @pl.loop(0, ROWS // 256)
        def _(i):
            part = pl.ds(pl.multiple_of(i * 256, 256), 256)
            term[s, part, :] = lax.dot_general(
                xin[s, :, part], cot[...], (((0,), (0,)), ((), ())), preferred_element_type=F32
            )

    def own_columns(r, start, size):
        return pl.ds(pl.multiple_of((yl * Z + lax.rem(z + Z - r, Z)) * ROWS + start, 128), size)

    def pair_columns(r, start, size):
        return pl.ds(pl.multiple_of(((1 - yl) * Z + lax.rem(z + Z - r, Z)) * ROWS + start, 128), size)

    def ig_sent(r):
        return remote(
            ig_far.at[r], ig_ref.at[0, :, own_columns(r, PURE, HYB)], yi_s.at[r], yi_r.at[r], pair
        )

    def ig_arrival(r):
        part = ig_ref.at[0, :, pair_columns(r, PURE, HYB)]
        return remote(part, part, yi_s.at[r], yi_r.at[r], pair)

    def make_ig(r):
        transposed = (((1,), (1,)), ((), ()))
        ig_far[r] = lax.dot_general(
            cot[TOK:, :], wb[r, PURE:ROWS, :], transposed, preferred_element_type=F32
        ).astype(BF16)
        ig_sent(r).start()
        ig_ref[0, :, own_columns(r, 0, ROWS)] = lax.dot_general(
            cot[:TOK, :], wb[r, :ROWS, :], transposed, preferred_element_type=F32
        ).astype(BF16)
        ig_ref[0, :, pair_columns(r, 0, PURE)] = lax.dot_general(
            cot[:TOK, :], wb[r, ROWS:, :], transposed, preferred_element_type=F32
        ).astype(BF16)

    def pass_on(r, i):
        for d in (UP, DOWN):
            c = 2 if i == 2 else (first[d] if i == 0 else 1 - first[d])
            gather(d, r, c).wait_recv()
            if r + 1 < 3:
                gather(d, r + 1, c).start()
            elif r + 1 == 3 and i == 0:
                gather(d, 3, c).start()
            elif r + 1 == 3 and i == 2:
                gather(d, 3, last_pure[d]).start()

    pl.semaphore_wait(barrier, 4 + len(plane))

    y_w.start()
    for d in (UP, DOWN):
        gather(d, 0, first[d]).start()
        gather(d, 0, 1 - first[d]).start()
    y_c.start()
    for s in (4, 3, 5, 2):
        y_x[s].start()
    for copy in c_1:
        copy.start()

    y_w.wait_recv()
    for d in (UP, DOWN):
        gather(d, 0, 2).start()
    pass_on(0, 0)
    for copy in local[:3]:
        copy.wait()
    total = pg_own[...].astype(F32)
    for j in range(1, PLANE):
        c_1[j - 1].wait_recv()
        total = total + c_in[j - 1].astype(F32)
    c_out[...] = total.astype(BF16)
    c_2.start()
    for s in (6, 1, 7, 0):
        y_x[s].start()
    y_c.wait_recv()
    make_ig(0)
    pass_on(0, 1)
    pass_on(0, 2)
    make_term(4)
    make_ig(1)
    make_ig(7)
    pass_on(1, 0)
    make_term(3)
    pass_on(1, 1)
    make_term(5)
    pass_on(1, 2)
    make_ig(2)
    make_ig(6)
    make_term(2)
    pass_on(2, 0)
    c_2.wait_recv()
    avg[own_piece, :] = (c_out[...].astype(F32) + c_far[...].astype(F32)) * (1.0 / 16)
    for copy in c_3:
        copy.start()
    make_term(6)
    pass_on(2, 1)
    pass_on(2, 2)
    for d in (UP, DOWN):
        send_sum(d, 4, half_of[d][0], False)
    for d in (UP, DOWN):
        send_sum(d, 3, half_of[d][1], False)
    make_ig(3)
    make_ig(5)
    make_term(1)
    for d in (UP, DOWN):
        gather(d, 3, first[d]).wait_recv()
        gather(d, 3, last_pure[d]).wait_recv()
    make_ig(4)
    make_term(7)
    for d in (UP, DOWN):
        send_sum(d, 3, half_of[d][0], True)
    make_term(0)
    for h in (1, 0):
        for d in (UP, DOWN):
            send_sum(d, 2, half_of[d][h], True)

    for copy in local[3:]:
        copy.wait()
    for j in range(1, PLANE):
        c_3_arrival(j).wait_recv()

    @pl.loop(0, ROWS // 64)
    def _(i):
        part = pl.ds(pl.multiple_of(i * 64, 64), 64)
        average = avg[part, :]
        momentum = outer_beta * omb[part, :] + average
        nm_ref[part, :] = momentum
        np_ref[part, :] = opb[part, :] - outer_rate * (average + outer_beta * momentum)

    for h in (1, 0):
        for d in (UP, DOWN):
            send_sum(d, 1, half_of[d][h], True)
    for d in (UP, DOWN):
        for h in (1, 0):
            reduce_copy(d, 1, half_of[d][h]).wait_recv()
    for h in (0, 1):
        part = rows(h * HALF, HALF)
        wg_ref[0, part, :] = (
            term[0, part, :] + rs_in[UP, 0, part, :].astype(F32) + rs_in[DOWN, 0, part, :].astype(F32)
        ) * (1.0 / 4096)

    for r in range(Z):
        ig_sent(r).wait_send()
    y_w.wait_send()
    y_c.wait_send()
    c_2.wait_send()
    for s in range(Z):
        y_x[s].wait_send()
    for j in range(1, PLANE):
        c_1[j - 1].wait_send()
        c_3[j - 1].wait_send()
    for d in (UP, DOWN):
        for r in range(3):
            for c in range(3):
                gather(d, r, c).wait_send()
        gather(d, 3, first[d]).wait_send()
        gather(d, 3, last_pure[d]).wait_send()
        reduce_copy(d, 4, half_of[d][0]).wait_send()
        for k in (3, 2, 1):
            for h in (0, 1):
                reduce_copy(d, k, h).wait_send()
    for r in range(Z):
        ig_arrival(r).wait_recv()


def finish_kernel(a, b, c, d, a_out, b_out, c_out, d_out, sems):
    copies = [pltpu.make_async_copy(x, y, sems.at[n]) for n, (x, y) in enumerate(
        [(a, a_out), (b, b_out), (c, c_out), (d, d_out)])]
    for copy in copies:
        copy.start()
    for copy in copies:
        copy.wait()


def finish(*arrays):
    return pl.pallas_call(
        finish_kernel,
        name="finish",
        out_shape=tuple(jax.ShapeDtypeStruct(x.shape, x.dtype) for x in arrays),
        in_specs=[pl.BlockSpec(memory_space=pltpu.VMEM)] * 4,
        out_specs=(pl.BlockSpec(memory_space=pltpu.HBM),) * 4,
        scratch_shapes=[pltpu.SemaphoreType.DMA((4,))],
        compiler_params=pltpu.CompilerParams(vmem_limit_bytes=2**20),
    )(*[pltpu.with_memory_space_constraint(x, pltpu.VMEM) for x in arrays])


def body(inputs, cotangent, key_weight, pseudo_grads, outer_params, outer_momentum):
    dma = pltpu.SemaphoreType.DMA
    vmem = pltpu.VMEM
    anywhere = pl.BlockSpec(memory_space=pltpu.HBM)
    return finish(*pl.pallas_call(
        kernel,
        name="key_backward",
        out_shape=(
            vmem((1, TOK, 2 * Z * ROWS), BF16),
            vmem((1, ROWS, KW), F32),
            vmem((ROWS, KW), F32),
            vmem((ROWS, KW), F32),
        ),
        in_specs=[anywhere] * 6,
        out_specs=(pl.BlockSpec(memory_space=vmem),) * 4,
        scratch_shapes=[
            vmem((2 * TOK, KW), BF16),
            vmem((Z, 2 * TOK, ROWS), BF16),
            vmem((Z, ROWS + PURE, KW), BF16),
            vmem((Z, ROWS, KW), F32),
            vmem((2, 4, ROWS, KW), BF16),
            vmem((2, 4, ROWS, KW), BF16),
            vmem((Z, TOK, HYB), BF16),
            vmem((PIECE, KW), BF16),
            vmem((PLANE - 1, PIECE, KW), BF16),
            vmem((PIECE, KW), BF16),
            vmem((PIECE, KW), BF16),
            vmem((ROWS, KW), F32),
            vmem((ROWS, KW), F32),
            vmem((ROWS, KW), F32),
            dma((2, 4, 3)), dma((2, 4, 3)),
            dma((2, 4, 2)), dma((2, 4, 2)),
            dma((Z,)), dma((Z,)),
            dma, dma, dma, dma,
            dma((Z,)), dma((Z,)),
            dma((PLANE - 1,)), dma((PLANE - 1,)),
            dma, dma,
            dma((PLANE - 1,)), dma((PLANE - 1,)),
            dma((Z,)), dma((5,)),
        ],
        compiler_params=pltpu.CompilerParams(
            collective_id=0, has_side_effects=True, vmem_limit_bytes=54 * 2**20
        ),
        cost_estimate=pl.CostEstimate(
            flops=4 * TOK * 2 * Z * ROWS * KW, bytes_accessed=24 * 2**20, transcendentals=0
        ),
    )(inputs, cotangent, key_weight, pseudo_grads, outer_params, outer_momentum))


def solution(mesh):
    return jax.shard_map(
        body,
        mesh=mesh,
        in_specs=(
            P("island", "fsdp", None),
            P("island", "fsdp", None),
            P("island", "fsdp", None),
            P("island", "fsdp", None),
            P("fsdp", None),
            P("fsdp", None),
        ),
        out_specs=(
            P("island", "fsdp", None),
            P("island", "fsdp", None),
            P("fsdp", None),
            P("fsdp", None),
        ),
        check_vma=False,
    )
```

```python
import functools

import jax
import jax.numpy as jnp
from jax import lax
from jax.experimental import pallas as pl
from jax.experimental.pallas import tpu as pltpu
from jax.sharding import PartitionSpec as P

outer_rate = 0.7
outer_beta = 0.9

MESH = pl.DeviceIdType.MESH
F32 = jnp.float32
BF16 = jnp.bfloat16

Z = 8
PLANE = 8
ROWS = 512
HALF = ROWS // 2
TOK = 256
PURE = 128
HYB = ROWS - PURE
KW = 512
PIECE = ROWS // PLANE

UP, DOWN = 0, 1


def rows(start, size):
    return pl.ds(start, size)


def kernel(
    x_ref, c_ref, w_ref, pg_ref, op_ref, om_ref,
    ig_ref, wg_ref, np_ref, nm_ref,
    cot, xin, wb, term, rs_in, rs_out, ig_far, ig_last,
    pg_own, c_in, c_out, c_far, avg, opb, omb,
    ag_s, ag_r, rs_s, rs_r, yx_s, yx_r, yc_s, yc_r, yw_s, yw_r, yi_s, yi_r,
    c1_s, c1_r, c2_s, c2_r, c3_s, c3_r, lx, lm,
):
    isl = lax.axis_index("island")
    fs = lax.axis_index("fsdp")
    z, yl = lax.rem(fs, Z), fs // Z
    q, yh = lax.rem(isl, PLANE), isl // PLANE
    up = (isl, yl * Z + lax.rem(z + 1, Z))
    down = (isl, yl * Z + lax.rem(z + Z - 1, Z))
    pair = (isl, (1 - yl) * Z + z)
    far = ((1 - yh) * PLANE + q, fs)
    plane = [(yh * PLANE + lax.rem(q + j, PLANE), fs) for j in range(1, PLANE)]
    ring = (up, down)

    barrier = pltpu.get_barrier_semaphore()
    for peer in [up, down, pair, far] + plane:
        pl.semaphore_signal(barrier, inc=1, device_id=peer, device_id_type=MESH)

    def remote(src, dst, ss, rs, peer):
        return pltpu.make_async_remote_copy(
            src_ref=src, dst_ref=dst, send_sem=ss, recv_sem=rs, device_id=peer, device_id_type=MESH
        )

    def columns(owner_yl, s):
        return pl.ds(pl.multiple_of((owner_yl * Z + lax.rem(z + s, Z)) * ROWS, ROWS), ROWS)

    local = [
        pltpu.make_async_copy(c_ref.at[0], cot.at[rows(0, TOK)], lm.at[0]),
        pltpu.make_async_copy(w_ref.at[0], wb.at[0, rows(0, ROWS)], lm.at[1]),
        pltpu.make_async_copy(
            pg_ref.at[0, pl.ds(pl.multiple_of(q * PIECE, PIECE), PIECE)], pg_own, lm.at[2]
        ),
        pltpu.make_async_copy(op_ref, opb, lm.at[3]),
        pltpu.make_async_copy(om_ref, omb, lm.at[4]),
    ]
    own_x = [
        pltpu.make_async_copy(x_ref.at[0, :, columns(yl, s)], xin.at[s, rows(0, TOK)], lx.at[s])
        for s in range(Z)
    ]
    y_w = remote(w_ref.at[0, rows(0, PURE)], wb.at[0, rows(ROWS, PURE)], yw_s, yw_r, pair)
    y_c = remote(c_ref.at[0], cot.at[rows(TOK, TOK)], yc_s, yc_r, pair)
    y_x = [
        remote(x_ref.at[0, :, columns(1 - yl, s)], xin.at[s, rows(TOK, TOK)], yx_s.at[s], yx_r.at[s], pair)
        for s in range(Z)
    ]

    cuts = {
        0: (0, HALF),
        1: (HALF, HALF),
        2: (ROWS, PURE),
    }

    def slot(d, r):
        return r if d == UP else (Z - r) % Z

    def gather(d, r, c):
        start, size = cuts[c]
        src = w_ref.at[0, rows(start, size)] if r == 0 and c < 2 else wb.at[slot(d, r), rows(start, size)]
        dst = wb.at[slot(d, r + 1), rows(start, size)]
        return remote(src, dst, ag_s.at[d, r, c], ag_r.at[d, r, c], ring[d])

    first = {UP: 0, DOWN: 1}

    c_1 = [
        remote(
            pg_ref.at[0, pl.ds(pl.multiple_of(lax.rem(q + j, PLANE) * PIECE, PIECE), PIECE)],
            c_in.at[j - 1], c1_s.at[j - 1], c1_r.at[j - 1], plane[j - 1],
        )
        for j in range(1, PLANE)
    ]
    c_2 = remote(c_out, c_far, c2_s, c2_r, far)
    own_piece = pl.ds(pl.multiple_of(q * PIECE, PIECE), PIECE)
    c_3 = [
        remote(avg.at[own_piece], avg.at[own_piece], c3_s.at[j - 1], c3_r.at[j - 1], plane[j - 1])
        for j in range(1, PLANE)
    ]

    def c_3_arrival(j):
        piece = pl.ds(pl.multiple_of(lax.rem(q + PLANE - j, PLANE) * PIECE, PIECE), PIECE)
        return remote(avg.at[piece], avg.at[piece], c3_s.at[j - 1], c3_r.at[j - 1], plane[j - 1])

    half_of = {UP: (0, 1), DOWN: (1, 0)}

    def reduce_copy(d, k, h):
        part = rows(h * HALF, HALF)
        return remote(
            rs_out.at[d, k - 1, part], rs_in.at[d, k - 1, part],
            rs_s.at[d, k - 1, h], rs_r.at[d, k - 1, h], ring[d],
        )

    def target(d, k):
        return k if d == UP else Z - k

    def send_sum(d, k, h, chained):
        part = rows(h * HALF, HALF)
        total = term[target(d, k), part, :]
        if chained:
            reduce_copy(d, k + 1, h).wait_recv()
            total = total + rs_in[d, k, part, :].astype(F32)
        rs_out[d, k - 1, part, :] = total.astype(BF16)
        reduce_copy(d, k, h).start()

    def make_term(s):
        own_x[s].wait()
        y_x[s].wait_recv()

        @pl.loop(0, ROWS // 256)
        def _(i):
            part = pl.ds(pl.multiple_of(i * 256, 256), 256)
            term[s, part, :] = lax.dot_general(
                xin[s, :, part], cot[...], (((0,), (0,)), ((), ())), preferred_element_type=F32
            )

    def own_columns(r, start, size):
        return pl.ds(pl.multiple_of((yl * Z + lax.rem(z + Z - r, Z)) * ROWS + start, 128), size)

    def pair_columns(r, start, size):
        return pl.ds(pl.multiple_of(((1 - yl) * Z + lax.rem(z + Z - r, Z)) * ROWS + start, 128), size)

    def far_part(r):
        return (0, ROWS, ig_last) if r == 4 else (PURE, HYB, ig_far.at[r])

    def ig_sent(r):
        start, size, src = far_part(r)
        return remote(
            src, ig_ref.at[0, :, own_columns(r, start, size)], yi_s.at[r], yi_r.at[r], pair
        )

    def ig_arrival(r):
        start, size, _ = far_part(r)
        part = ig_ref.at[0, :, pair_columns(r, start, size)]
        return remote(part, part, yi_s.at[r], yi_r.at[r], pair)

    def make_ig(r):
        transposed = (((1,), (1,)), ((), ()))
        start, size, far_ref = far_part(r)
        far_ref[...] = lax.dot_general(
            cot[TOK:, :], wb[r, start:ROWS, :], transposed, preferred_element_type=F32
        ).astype(BF16)
        ig_sent(r).start()
        ig_ref[0, :, own_columns(r, 0, ROWS)] = lax.dot_general(
            cot[:TOK, :], wb[r, :ROWS, :], transposed, preferred_element_type=F32
        ).astype(BF16)
        if r != 4:
            ig_ref[0, :, pair_columns(r, 0, PURE)] = lax.dot_general(
                cot[:TOK, :], wb[r, ROWS:, :], transposed, preferred_element_type=F32
            ).astype(BF16)

    def pass_on(r, i):
        for d in (UP, DOWN):
            c = 2 if i == 2 else (first[d] if i == 0 else 1 - first[d])
            gather(d, r, c).wait_recv()
            if r + 1 < 3:
                gather(d, r + 1, c).start()
            elif r + 1 == 3 and i == 0:
                gather(d, 3, c).start()

    pl.semaphore_wait(barrier, 4 + len(plane))

    y_w.start()
    for d in (UP, DOWN):
        gather(d, 0, first[d]).start()
        gather(d, 0, 1 - first[d]).start()
    y_c.start()
    for s in (4, 3, 5, 2):
        y_x[s].start()
    for copy in c_1:
        copy.start()
    for copy in local:
        copy.start()
    for s in (4, 3, 5, 2, 6, 1, 7, 0):
        own_x[s].start()

    y_w.wait_recv()
    for d in (UP, DOWN):
        gather(d, 0, 2).start()
    pass_on(0, 0)
    for copy in local[:3]:
        copy.wait()
    total = pg_own[...].astype(F32)
    for j in range(1, PLANE):
        c_1[j - 1].wait_recv()
        total = total + c_in[j - 1].astype(F32)
    c_out[...] = total.astype(BF16)
    c_2.start()
    for s in (6, 1, 7, 0):
        y_x[s].start()
    y_c.wait_recv()
    make_ig(0)
    pass_on(0, 1)
    pass_on(0, 2)
    make_term(4)
    make_ig(1)
    make_ig(7)
    pass_on(1, 0)
    make_term(3)
    pass_on(1, 1)
    make_term(5)
    pass_on(1, 2)
    make_ig(2)
    make_ig(6)
    make_term(2)
    pass_on(2, 0)
    c_2.wait_recv()
    avg[own_piece, :] = (c_out[...].astype(F32) + c_far[...].astype(F32)) * (1.0 / 16)
    for copy in c_3:
        copy.start()
    make_term(6)
    pass_on(2, 1)
    pass_on(2, 2)
    for d in (UP, DOWN):
        send_sum(d, 4, half_of[d][0], False)
    for d in (UP, DOWN):
        send_sum(d, 3, half_of[d][1], False)
    make_ig(3)
    make_ig(5)
    make_term(1)
    for d in (UP, DOWN):
        gather(d, 3, first[d]).wait_recv()
    make_ig(4)
    make_term(7)
    for d in (UP, DOWN):
        send_sum(d, 3, half_of[d][0], True)
    make_term(0)
    for h in (1, 0):
        for d in (UP, DOWN):
            send_sum(d, 2, half_of[d][h], True)

    for copy in local[3:]:
        copy.wait()
    for j in range(1, PLANE):
        c_3_arrival(j).wait_recv()

    @pl.loop(0, ROWS // 64)
    def _(i):
        part = pl.ds(pl.multiple_of(i * 64, 64), 64)
        average = avg[part, :]
        momentum = outer_beta * omb[part, :] + average
        nm_ref[part, :] = momentum
        np_ref[part, :] = opb[part, :] - outer_rate * (average + outer_beta * momentum)

    for h in (1, 0):
        for d in (UP, DOWN):
            send_sum(d, 1, half_of[d][h], True)

    y_w.wait_send()
    y_c.wait_send()
    c_2.wait_send()
    for s in range(Z):
        y_x[s].wait_send()
    for j in range(1, PLANE):
        c_1[j - 1].wait_send()
        c_3[j - 1].wait_send()
    for d in (UP, DOWN):
        for r in range(3):
            for c in range(3):
                gather(d, r, c).wait_send()
        gather(d, 3, first[d]).wait_send()
        reduce_copy(d, 4, half_of[d][0]).wait_send()
        for k in (3, 2):
            for h in (0, 1):
                reduce_copy(d, k, h).wait_send()
    for r in (0, 1, 7, 2, 6):
        ig_sent(r).wait_send()
        ig_arrival(r).wait_recv()

    for d in (UP, DOWN):
        for h in (1, 0):
            reduce_copy(d, 1, half_of[d][h]).wait_recv()
    for h in (0, 1):
        part = rows(h * HALF, HALF)
        wg_ref[0, part, :] = (
            term[0, part, :] + rs_in[UP, 0, part, :].astype(F32) + rs_in[DOWN, 0, part, :].astype(F32)
        ) * (1.0 / 4096)

    for d in (UP, DOWN):
        for h in (0, 1):
            reduce_copy(d, 1, h).wait_send()
    for r in (3, 5, 4):
        ig_sent(r).wait_send()
        ig_arrival(r).wait_recv()


def finish_kernel(a, b, c, d, a_out, b_out, c_out, d_out, sems):
    copies = [pltpu.make_async_copy(x, y, sems.at[n]) for n, (x, y) in enumerate(
        [(a, a_out), (b, b_out), (c, c_out), (d, d_out)])]
    for copy in copies:
        copy.start()
    for copy in copies:
        copy.wait()


def finish(*arrays):
    return pl.pallas_call(
        finish_kernel,
        name="finish",
        out_shape=tuple(jax.ShapeDtypeStruct(x.shape, x.dtype) for x in arrays),
        in_specs=[pl.BlockSpec(memory_space=pltpu.VMEM)] * 4,
        out_specs=(pl.BlockSpec(memory_space=pltpu.HBM),) * 4,
        scratch_shapes=[pltpu.SemaphoreType.DMA((4,))],
        compiler_params=pltpu.CompilerParams(vmem_limit_bytes=2**20),
    )(*[pltpu.with_memory_space_constraint(x, pltpu.VMEM) for x in arrays])


def body(inputs, cotangent, key_weight, pseudo_grads, outer_params, outer_momentum):
    dma = pltpu.SemaphoreType.DMA
    vmem = pltpu.VMEM
    anywhere = pl.BlockSpec(memory_space=pltpu.HBM)
    return finish(*pl.pallas_call(
        kernel,
        name="key_backward",
        out_shape=(
            vmem((1, TOK, 2 * Z * ROWS), BF16),
            vmem((1, ROWS, KW), F32),
            vmem((ROWS, KW), F32),
            vmem((ROWS, KW), F32),
        ),
        in_specs=[anywhere] * 6,
        out_specs=(pl.BlockSpec(memory_space=vmem),) * 4,
        scratch_shapes=[
            vmem((2 * TOK, KW), BF16),
            vmem((Z, 2 * TOK, ROWS), BF16),
            vmem((Z, ROWS + PURE, KW), BF16),
            vmem((Z, ROWS, KW), F32),
            vmem((2, 4, ROWS, KW), BF16),
            vmem((2, 4, ROWS, KW), BF16),
            vmem((Z, TOK, HYB), BF16),
            vmem((TOK, ROWS), BF16),
            vmem((PIECE, KW), BF16),
            vmem((PLANE - 1, PIECE, KW), BF16),
            vmem((PIECE, KW), BF16),
            vmem((PIECE, KW), BF16),
            vmem((ROWS, KW), F32),
            vmem((ROWS, KW), F32),
            vmem((ROWS, KW), F32),
            dma((2, 4, 3)), dma((2, 4, 3)),
            dma((2, 4, 2)), dma((2, 4, 2)),
            dma((Z,)), dma((Z,)),
            dma, dma, dma, dma,
            dma((Z,)), dma((Z,)),
            dma((PLANE - 1,)), dma((PLANE - 1,)),
            dma, dma,
            dma((PLANE - 1,)), dma((PLANE - 1,)),
            dma((Z,)), dma((5,)),
        ],
        compiler_params=pltpu.CompilerParams(
            collective_id=0, has_side_effects=True, vmem_limit_bytes=54 * 2**20
        ),
        cost_estimate=pl.CostEstimate(
            flops=4 * TOK * 2 * Z * ROWS * KW, bytes_accessed=24 * 2**20, transcendentals=0
        ),
    )(inputs, cotangent, key_weight, pseudo_grads, outer_params, outer_momentum))


def solution(mesh):
    return jax.shard_map(
        body,
        mesh=mesh,
        in_specs=(
            P("island", "fsdp", None),
            P("island", "fsdp", None),
            P("island", "fsdp", None),
            P("island", "fsdp", None),
            P("fsdp", None),
            P("fsdp", None),
        ),
        out_specs=(
            P("island", "fsdp", None),
            P("island", "fsdp", None),
            P("fsdp", None),
            P("fsdp", None),
        ),
        check_vma=False,
    )
```

```python
import functools

import jax
import jax.numpy as jnp
from jax import lax
from jax.experimental import pallas as pl
from jax.experimental.pallas import tpu as pltpu
from jax.sharding import PartitionSpec as P

outer_rate = 0.7
outer_beta = 0.9

MESH = pl.DeviceIdType.MESH
F32 = jnp.float32
BF16 = jnp.bfloat16

Z = 8
PLANE = 8
ROWS = 512
HALF = ROWS // 2
TOK = 256
PURE = 128
HYB = ROWS - PURE
KW = 512
PIECE = ROWS // PLANE

UP, DOWN = 0, 1
ISLANDS = 2 * PLANE
ROOT = 1


def rows(start, size):
    return pl.ds(start, size)


def kernel(
    x_ref, c_ref, w_ref, pg_ref, op_ref, om_ref,
    ig_ref, wg_ref, np_ref, nm_ref,
    cot, xin, wb, term, rs_in, rs_out, ig_far, ig_last,
    pg_own, c_in, c_out, c_far, avg, opb, omb,
    ag_s, ag_r, rs_s, rs_r, yx_s, yx_r, yc_s, yc_r, yw_s, yw_r, yi_s, yi_r,
    c1_s, c1_r, c2_s, c2_r, c3_s, c3_r, lx, lm, below, here, all_in,
):
    isl = lax.axis_index("island")
    fs = lax.axis_index("fsdp")
    z, yl = lax.rem(fs, Z), fs // Z
    q, yh = lax.rem(isl, PLANE), isl // PLANE
    up = (isl, yl * Z + lax.rem(z + 1, Z))
    down = (isl, yl * Z + lax.rem(z + Z - 1, Z))
    pair = (isl, (1 - yl) * Z + z)
    far = ((1 - yh) * PLANE + q, fs)
    plane = [(yh * PLANE + lax.rem(q + j, PLANE), fs) for j in range(1, PLANE)]
    ring = (up, down)

    barrier = pltpu.get_barrier_semaphore()
    for peer in (down, pair):
        pl.semaphore_signal(barrier, inc=1, device_id=peer, device_id_type=MESH)

    @pl.when(isl == ROOT)
    def _():
        for j in range(1, ISLANDS):
            pl.semaphore_signal(
                barrier, inc=1, device_id=(lax.rem(isl + j, ISLANDS), fs), device_id_type=MESH
            )

    def remote(src, dst, ss, rs, peer):
        return pltpu.make_async_remote_copy(
            src_ref=src, dst_ref=dst, send_sem=ss, recv_sem=rs, device_id=peer, device_id_type=MESH
        )

    def columns(owner_yl, s):
        return pl.ds(pl.multiple_of((owner_yl * Z + lax.rem(z + s, Z)) * ROWS, ROWS), ROWS)

    local = [
        pltpu.make_async_copy(c_ref.at[0], cot.at[rows(0, TOK)], lm.at[0]),
        pltpu.make_async_copy(w_ref.at[0], wb.at[0, rows(0, ROWS)], lm.at[1]),
        pltpu.make_async_copy(
            pg_ref.at[0, pl.ds(pl.multiple_of(q * PIECE, PIECE), PIECE)], pg_own, lm.at[2]
        ),
        pltpu.make_async_copy(op_ref, opb, lm.at[3]),
        pltpu.make_async_copy(om_ref, omb, lm.at[4]),
    ]
    own_x = [
        pltpu.make_async_copy(x_ref.at[0, :, columns(yl, s)], xin.at[s, rows(0, TOK)], lx.at[s])
        for s in range(Z)
    ]
    y_w = remote(w_ref.at[0, rows(0, PURE)], wb.at[0, rows(ROWS, PURE)], yw_s, yw_r, pair)
    y_c = remote(c_ref.at[0], cot.at[rows(TOK, TOK)], yc_s, yc_r, pair)
    y_x = [
        remote(x_ref.at[0, :, columns(1 - yl, s)], xin.at[s, rows(TOK, TOK)], yx_s.at[s], yx_r.at[s], pair)
        for s in range(Z)
    ]

    cuts = {
        0: (0, HALF),
        1: (HALF, HALF),
        2: (ROWS, PURE),
    }

    def slot(d, r):
        return r if d == UP else (Z - r) % Z

    def gather(d, r, c):
        start, size = cuts[c]
        src = w_ref.at[0, rows(start, size)] if r == 0 and c < 2 else wb.at[slot(d, r), rows(start, size)]
        dst = wb.at[slot(d, r + 1), rows(start, size)]
        return remote(src, dst, ag_s.at[d, r, c], ag_r.at[d, r, c], ring[d])

    first = {UP: 0, DOWN: 1}

    c_1 = [
        remote(
            pg_ref.at[0, pl.ds(pl.multiple_of(lax.rem(q + j, PLANE) * PIECE, PIECE), PIECE)],
            c_in.at[j - 1], c1_s.at[j - 1], c1_r.at[j - 1], plane[j - 1],
        )
        for j in range(1, PLANE)
    ]
    c_2 = remote(c_out, c_far, c2_s, c2_r, far)
    own_piece = pl.ds(pl.multiple_of(q * PIECE, PIECE), PIECE)
    c_3 = [
        remote(avg.at[own_piece], avg.at[own_piece], c3_s.at[j - 1], c3_r.at[j - 1], plane[j - 1])
        for j in range(1, PLANE)
    ]

    def c_3_arrival(j):
        piece = pl.ds(pl.multiple_of(lax.rem(q + PLANE - j, PLANE) * PIECE, PIECE), PIECE)
        return remote(avg.at[piece], avg.at[piece], c3_s.at[j - 1], c3_r.at[j - 1], plane[j - 1])

    half_of = {UP: (0, 1), DOWN: (1, 0)}

    def reduce_copy(d, k, h):
        part = rows(h * HALF, HALF)
        return remote(
            rs_out.at[d, k - 1, part], rs_in.at[d, k - 1, part],
            rs_s.at[d, k - 1, h], rs_r.at[d, k - 1, h], ring[d],
        )

    def target(d, k):
        return k if d == UP else Z - k

    def send_sum(d, k, h, chained):
        part = rows(h * HALF, HALF)
        total = term[target(d, k), part, :]
        if chained:
            reduce_copy(d, k + 1, h).wait_recv()
            total = total + rs_in[d, k, part, :].astype(F32)
        rs_out[d, k - 1, part, :] = total.astype(BF16)
        reduce_copy(d, k, h).start()

    def make_term(s):
        own_x[s].wait()
        y_x[s].wait_recv()

        @pl.loop(0, ROWS // 256)
        def _(i):
            part = pl.ds(pl.multiple_of(i * 256, 256), 256)
            term[s, part, :] = lax.dot_general(
                xin[s, :, part], cot[...], (((0,), (0,)), ((), ())), preferred_element_type=F32
            )

    def own_columns(r, start, size):
        return pl.ds(pl.multiple_of((yl * Z + lax.rem(z + Z - r, Z)) * ROWS + start, 128), size)

    def pair_columns(r, start, size):
        return pl.ds(pl.multiple_of(((1 - yl) * Z + lax.rem(z + Z - r, Z)) * ROWS + start, 128), size)

    def far_part(r):
        return (0, ROWS, ig_last) if r == 4 else (PURE, HYB, ig_far.at[r])

    def ig_sent(r):
        start, size, src = far_part(r)
        return remote(
            src, ig_ref.at[0, :, own_columns(r, start, size)], yi_s.at[r], yi_r.at[r], pair
        )

    def ig_arrival(r):
        start, size, _ = far_part(r)
        part = ig_ref.at[0, :, pair_columns(r, start, size)]
        return remote(part, part, yi_s.at[r], yi_r.at[r], pair)

    def make_ig(r):
        transposed = (((1,), (1,)), ((), ()))
        start, size, far_ref = far_part(r)
        far_ref[...] = lax.dot_general(
            cot[TOK:, :], wb[r, start:ROWS, :], transposed, preferred_element_type=F32
        ).astype(BF16)
        ig_sent(r).start()
        ig_ref[0, :, own_columns(r, 0, ROWS)] = lax.dot_general(
            cot[:TOK, :], wb[r, :ROWS, :], transposed, preferred_element_type=F32
        ).astype(BF16)
        if r != 4:
            ig_ref[0, :, pair_columns(r, 0, PURE)] = lax.dot_general(
                cot[:TOK, :], wb[r, ROWS:, :], transposed, preferred_element_type=F32
            ).astype(BF16)

    def pass_on(r, i):
        for d in (UP, DOWN):
            c = 2 if i == 2 else (first[d] if i == 0 else 1 - first[d])
            gather(d, r, c).wait_recv()
            if r + 1 < 3:
                gather(d, r + 1, c).start()
            elif r + 1 == 3 and i == 0:
                gather(d, 3, c).start()

    pl.semaphore_wait(barrier, jnp.where(isl == ROOT, 2, 3))
    pl.semaphore_signal(below, inc=1, device_id=up, device_id_type=MESH)
    y_w.start()
    gather(UP, 0, first[UP]).start()
    gather(UP, 0, 1 - first[UP]).start()
    y_c.start()
    for s in (4, 3, 5, 2):
        y_x[s].start()

    @pl.when(isl != ROOT)
    def _():
        pl.semaphore_signal(here, inc=1, device_id=(ROOT, fs), device_id_type=MESH)

    for copy in local:
        copy.start()
    for s in (4, 3, 5, 2, 6, 1, 7, 0):
        own_x[s].start()
    pl.semaphore_wait(below, 1)
    gather(DOWN, 0, first[DOWN]).start()
    gather(DOWN, 0, 1 - first[DOWN]).start()

    @pl.when(isl == ROOT)
    def _():
        pl.semaphore_wait(here, ISLANDS - 1)
        for j in range(1, ISLANDS):
            pl.semaphore_signal(
                all_in, inc=1, device_id=(lax.rem(isl + j, ISLANDS), fs), device_id_type=MESH
            )

    @pl.when(isl != ROOT)
    def _():
        pl.semaphore_wait(all_in, 1)

    for copy in c_1:
        copy.start()
    y_w.wait_recv()
    for d in (UP, DOWN):
        gather(d, 0, 2).start()
    pass_on(0, 0)
    for copy in local[:3]:
        copy.wait()
    total = pg_own[...].astype(F32)
    for j in range(1, PLANE):
        c_1[j - 1].wait_recv()
        total = total + c_in[j - 1].astype(F32)
    c_out[...] = total.astype(BF16)
    c_2.start()
    for s in (6, 1, 7, 0):
        y_x[s].start()
    y_c.wait_recv()
    make_ig(0)
    pass_on(0, 1)
    pass_on(0, 2)
    make_term(4)
    make_ig(1)
    make_ig(7)
    pass_on(1, 0)
    make_term(3)
    pass_on(1, 1)
    make_term(5)
    pass_on(1, 2)
    make_ig(2)
    make_ig(6)
    make_term(2)
    pass_on(2, 0)
    c_2.wait_recv()
    avg[own_piece, :] = (c_out[...].astype(F32) + c_far[...].astype(F32)) * (1.0 / 16)
    for copy in c_3:
        copy.start()
    make_term(6)
    pass_on(2, 1)
    pass_on(2, 2)
    for d in (UP, DOWN):
        send_sum(d, 4, half_of[d][0], False)
    for d in (UP, DOWN):
        send_sum(d, 3, half_of[d][1], False)
    make_ig(3)
    make_ig(5)
    make_term(1)
    for d in (UP, DOWN):
        gather(d, 3, first[d]).wait_recv()
    make_ig(4)
    make_term(7)
    for d in (UP, DOWN):
        send_sum(d, 3, half_of[d][0], True)
    make_term(0)
    for h in (1, 0):
        for d in (UP, DOWN):
            send_sum(d, 2, half_of[d][h], True)

    for copy in local[3:]:
        copy.wait()
    for j in range(1, PLANE):
        c_3_arrival(j).wait_recv()

    @pl.loop(0, ROWS // 64)
    def _(i):
        part = pl.ds(pl.multiple_of(i * 64, 64), 64)
        average = avg[part, :]
        momentum = outer_beta * omb[part, :] + average
        nm_ref[part, :] = momentum
        np_ref[part, :] = opb[part, :] - outer_rate * (average + outer_beta * momentum)

    for h in (1, 0):
        for d in (UP, DOWN):
            send_sum(d, 1, half_of[d][h], True)

    y_w.wait_send()
    y_c.wait_send()
    c_2.wait_send()
    for s in range(Z):
        y_x[s].wait_send()
    for j in range(1, PLANE):
        c_1[j - 1].wait_send()
        c_3[j - 1].wait_send()
    for d in (UP, DOWN):
        for r in range(3):
            for c in range(3):
                gather(d, r, c).wait_send()
        gather(d, 3, first[d]).wait_send()
        reduce_copy(d, 4, half_of[d][0]).wait_send()
        for k in (3, 2):
            for h in (0, 1):
                reduce_copy(d, k, h).wait_send()
    for r in (0, 1, 7, 2, 6):
        ig_sent(r).wait_send()
        ig_arrival(r).wait_recv()

    for d in (UP, DOWN):
        for h in (1, 0):
            reduce_copy(d, 1, half_of[d][h]).wait_recv()
    for h in (0, 1):
        part = rows(h * HALF, HALF)
        wg_ref[0, part, :] = (
            term[0, part, :] + rs_in[UP, 0, part, :].astype(F32) + rs_in[DOWN, 0, part, :].astype(F32)
        ) * (1.0 / 4096)

    for d in (UP, DOWN):
        for h in (0, 1):
            reduce_copy(d, 1, h).wait_send()
    for r in (3, 5, 4):
        ig_sent(r).wait_send()
        ig_arrival(r).wait_recv()


def finish_kernel(a, b, c, d, a_out, b_out, c_out, d_out, sems):
    copies = [pltpu.make_async_copy(x, y, sems.at[n]) for n, (x, y) in enumerate(
        [(a, a_out), (b, b_out), (c, c_out), (d, d_out)])]
    for copy in copies:
        copy.start()
    for copy in copies:
        copy.wait()


def finish(*arrays):
    return pl.pallas_call(
        finish_kernel,
        name="finish",
        out_shape=tuple(jax.ShapeDtypeStruct(x.shape, x.dtype) for x in arrays),
        in_specs=[pl.BlockSpec(memory_space=pltpu.VMEM)] * 4,
        out_specs=(pl.BlockSpec(memory_space=pltpu.HBM),) * 4,
        scratch_shapes=[pltpu.SemaphoreType.DMA((4,))],
        compiler_params=pltpu.CompilerParams(vmem_limit_bytes=2**20),
    )(*[pltpu.with_memory_space_constraint(x, pltpu.VMEM) for x in arrays])


def body(inputs, cotangent, key_weight, pseudo_grads, outer_params, outer_momentum):
    dma = pltpu.SemaphoreType.DMA
    vmem = pltpu.VMEM
    anywhere = pl.BlockSpec(memory_space=pltpu.HBM)
    return finish(*pl.pallas_call(
        kernel,
        name="key_backward",
        out_shape=(
            vmem((1, TOK, 2 * Z * ROWS), BF16),
            vmem((1, ROWS, KW), F32),
            vmem((ROWS, KW), F32),
            vmem((ROWS, KW), F32),
        ),
        in_specs=[anywhere] * 6,
        out_specs=(pl.BlockSpec(memory_space=vmem),) * 4,
        scratch_shapes=[
            vmem((2 * TOK, KW), BF16),
            vmem((Z, 2 * TOK, ROWS), BF16),
            vmem((Z, ROWS + PURE, KW), BF16),
            vmem((Z, ROWS, KW), F32),
            vmem((2, 4, ROWS, KW), BF16),
            vmem((2, 4, ROWS, KW), BF16),
            vmem((Z, TOK, HYB), BF16),
            vmem((TOK, ROWS), BF16),
            vmem((PIECE, KW), BF16),
            vmem((PLANE - 1, PIECE, KW), BF16),
            vmem((PIECE, KW), BF16),
            vmem((PIECE, KW), BF16),
            vmem((ROWS, KW), F32),
            vmem((ROWS, KW), F32),
            vmem((ROWS, KW), F32),
            dma((2, 4, 3)), dma((2, 4, 3)),
            dma((2, 4, 2)), dma((2, 4, 2)),
            dma((Z,)), dma((Z,)),
            dma, dma, dma, dma,
            dma((Z,)), dma((Z,)),
            dma((PLANE - 1,)), dma((PLANE - 1,)),
            dma, dma,
            dma((PLANE - 1,)), dma((PLANE - 1,)),
            dma((Z,)), dma((5,)),
            pltpu.SemaphoreType.REGULAR,
            pltpu.SemaphoreType.REGULAR,
            pltpu.SemaphoreType.REGULAR,
        ],
        compiler_params=pltpu.CompilerParams(
            collective_id=0, has_side_effects=True, vmem_limit_bytes=54 * 2**20
        ),
        cost_estimate=pl.CostEstimate(
            flops=4 * TOK * 2 * Z * ROWS * KW, bytes_accessed=24 * 2**20, transcendentals=0
        ),
    )(inputs, cotangent, key_weight, pseudo_grads, outer_params, outer_momentum))


def solution(mesh):
    return jax.shard_map(
        body,
        mesh=mesh,
        in_specs=(
            P("island", "fsdp", None),
            P("island", "fsdp", None),
            P("island", "fsdp", None),
            P("island", "fsdp", None),
            P("fsdp", None),
            P("fsdp", None),
        ),
        out_specs=(
            P("island", "fsdp", None),
            P("island", "fsdp", None),
            P("fsdp", None),
            P("fsdp", None),
        ),
        check_vma=False,
    )
```

```python
import functools

import jax
import jax.numpy as jnp
from jax import lax
from jax.experimental import pallas as pl
from jax.experimental.pallas import tpu as pltpu
from jax.sharding import PartitionSpec as P

outer_rate = 0.7
outer_beta = 0.9

MESH = pl.DeviceIdType.MESH
F32 = jnp.float32
BF16 = jnp.bfloat16

Z = 8
PLANE = 8
ROWS = 512
HALF = ROWS // 2
TOK = 256
PURE = 128
HYB = ROWS - PURE
KW = 512
PIECE = ROWS // PLANE

UP, DOWN = 0, 1
ISLANDS = 2 * PLANE
SIDE = 96
ROOT = 1


def rows(start, size):
    return pl.ds(start, size)


def kernel(
    x_ref, c_ref, w_ref, pg_ref, op_ref, om_ref,
    ig_ref, wg_ref, np_ref, nm_ref,
    cot, xin, wb, term, rs_in, rs_out, ig_far, ig_last,
    pg_own, c_in, c_out, c_far, avg, opb, omb,
    ag_s, ag_r, rs_s, rs_r, yx_s, yx_r, yc_s, yc_r, yw_s, yw_r, yi_s, yi_r,
    c1_s, c1_r, c2_s, c2_r, c3_s, c3_r, lx, lm, above, below, pair_in, here, all_in,
):
    isl = lax.axis_index("island")
    fs = lax.axis_index("fsdp")
    z, yl = lax.rem(fs, Z), fs // Z
    q, yh = lax.rem(isl, PLANE), isl // PLANE
    up = (isl, yl * Z + lax.rem(z + 1, Z))
    down = (isl, yl * Z + lax.rem(z + Z - 1, Z))
    pair = (isl, (1 - yl) * Z + z)
    far = ((1 - yh) * PLANE + q, fs)
    plane = [(yh * PLANE + lax.rem(q + j, PLANE), fs) for j in range(1, PLANE)]
    ring = (up, down)

    barrier = pltpu.get_barrier_semaphore()
    def greet(sem, peer):
        pl.semaphore_signal(sem, inc=1, device_id=peer, device_id_type=MESH)

    pl.when(yl == 0)(lambda: greet(barrier, pair))
    greet(barrier, (isl, fs))
    pl.when(z < Z - 1)(lambda: greet(barrier, up))
    pl.when(z == 0)(lambda: greet(barrier, down))

    @pl.when(isl == ROOT)
    def _():
        for j in range(1, ISLANDS):
            greet(barrier, (lax.rem(isl + j, ISLANDS), fs))

    def count(condition):
        return jnp.where(condition, 1, 0)

    def remote(src, dst, ss, rs, peer):
        return pltpu.make_async_remote_copy(
            src_ref=src, dst_ref=dst, send_sem=ss, recv_sem=rs, device_id=peer, device_id_type=MESH
        )

    def columns(owner_yl, s):
        return pl.ds(pl.multiple_of((owner_yl * Z + lax.rem(z + s, Z)) * ROWS, ROWS), ROWS)

    local = [
        pltpu.make_async_copy(c_ref.at[0], cot.at[rows(0, TOK)], lm.at[0]),
        pltpu.make_async_copy(w_ref.at[0], wb.at[0, rows(0, ROWS)], lm.at[1]),
        pltpu.make_async_copy(
            pg_ref.at[0, pl.ds(pl.multiple_of(q * PIECE, PIECE), PIECE)], pg_own, lm.at[2]
        ),
        pltpu.make_async_copy(op_ref, opb, lm.at[3]),
        pltpu.make_async_copy(om_ref, omb, lm.at[4]),
    ]
    own_x = [
        pltpu.make_async_copy(x_ref.at[0, :, columns(yl, s)], xin.at[s, rows(0, TOK)], lx.at[s])
        for s in range(Z)
    ]
    y_w = remote(w_ref.at[0, rows(0, PURE)], wb.at[0, rows(ROWS, PURE)], yw_s, yw_r, pair)
    y_c = remote(c_ref.at[0], cot.at[rows(TOK, TOK)], yc_s, yc_r, pair)
    y_x = [
        remote(x_ref.at[0, :, columns(1 - yl, s)], xin.at[s, rows(TOK, TOK)], yx_s.at[s], yx_r.at[s], pair)
        for s in range(Z)
    ]

    cuts = {
        0: (0, HALF),
        1: (HALF, HALF),
        2: (ROWS, PURE),
    }

    def slot(d, r):
        return r if d == UP else (Z - r) % Z

    def gather(d, r, c):
        start, size = cuts[c]
        src = w_ref.at[0, rows(start, size)] if r == 0 and c < 2 else wb.at[slot(d, r), rows(start, size)]
        dst = wb.at[slot(d, r + 1), rows(start, size)]
        return remote(src, dst, ag_s.at[d, r, c], ag_r.at[d, r, c], ring[d])

    first = {UP: 0, DOWN: 1}

    last_hop = {
        UP: (
            (0, HALF - SIDE, None, None),
            (HALF - SIDE, SIDE, z < Z - 1, z > 0),
            (HALF, SIDE, z == Z - 2, z == Z - 1),
        ),
        DOWN: (
            (HALF + SIDE, HALF - SIDE, None, None),
            (HALF, SIDE, z > 0, z < Z - 1),
            (HALF - SIDE, SIDE, z == 1, z == 0),
        ),
    }

    def fourth(d, c):
        start, size = last_hop[d][c][:2]
        return remote(
            wb.at[slot(d, 3), rows(start, size)], wb.at[4, rows(start, size)],
            ag_s.at[d, 3, c], ag_r.at[d, 3, c], ring[d],
        )

    def only(condition, action):
        if condition is None:
            action()
        else:
            pl.when(condition)(action)

    def fourth_start(d, c):
        only(last_hop[d][c][2], lambda: fourth(d, c).start())

    c_1 = [
        remote(
            pg_ref.at[0, pl.ds(pl.multiple_of(lax.rem(q + j, PLANE) * PIECE, PIECE), PIECE)],
            c_in.at[j - 1], c1_s.at[j - 1], c1_r.at[j - 1], plane[j - 1],
        )
        for j in range(1, PLANE)
    ]
    c_2 = remote(c_out, c_far, c2_s, c2_r, far)
    own_piece = pl.ds(pl.multiple_of(q * PIECE, PIECE), PIECE)
    c_3 = [
        remote(avg.at[own_piece], avg.at[own_piece], c3_s.at[j - 1], c3_r.at[j - 1], plane[j - 1])
        for j in range(1, PLANE)
    ]

    def c_3_arrival(j):
        piece = pl.ds(pl.multiple_of(lax.rem(q + PLANE - j, PLANE) * PIECE, PIECE), PIECE)
        return remote(avg.at[piece], avg.at[piece], c3_s.at[j - 1], c3_r.at[j - 1], plane[j - 1])

    half_of = {UP: (0, 1), DOWN: (1, 0)}

    def reduce_copy(d, k, h):
        part = rows(h * HALF, HALF)
        return remote(
            rs_out.at[d, k - 1, part], rs_in.at[d, k - 1, part],
            rs_s.at[d, k - 1, h], rs_r.at[d, k - 1, h], ring[d],
        )

    def target(d, k):
        return k if d == UP else Z - k

    def send_sum(d, k, h, chained):
        part = rows(h * HALF, HALF)
        total = term[target(d, k), part, :]
        if chained:
            reduce_copy(d, k + 1, h).wait_recv()
            total = total + rs_in[d, k, part, :].astype(F32)
        rs_out[d, k - 1, part, :] = total.astype(BF16)
        reduce_copy(d, k, h).start()

    def make_term(s):
        own_x[s].wait()
        y_x[s].wait_recv()

        @pl.loop(0, ROWS // 256)
        def _(i):
            part = pl.ds(pl.multiple_of(i * 256, 256), 256)
            term[s, part, :] = lax.dot_general(
                xin[s, :, part], cot[...], (((0,), (0,)), ((), ())), preferred_element_type=F32
            )

    def own_columns(r, start, size):
        return pl.ds(pl.multiple_of((yl * Z + lax.rem(z + Z - r, Z)) * ROWS + start, 128), size)

    def pair_columns(r, start, size):
        return pl.ds(pl.multiple_of(((1 - yl) * Z + lax.rem(z + Z - r, Z)) * ROWS + start, 128), size)

    def far_part(r):
        return (0, ROWS, ig_last) if r == 4 else (PURE, HYB, ig_far.at[r])

    def ig_sent(r):
        start, size, src = far_part(r)
        return remote(
            src, ig_ref.at[0, :, own_columns(r, start, size)], yi_s.at[r], yi_r.at[r], pair
        )

    def ig_arrival(r):
        start, size, _ = far_part(r)
        part = ig_ref.at[0, :, pair_columns(r, start, size)]
        return remote(part, part, yi_s.at[r], yi_r.at[r], pair)

    def make_ig(r):
        transposed = (((1,), (1,)), ((), ()))
        start, size, far_ref = far_part(r)
        far_ref[...] = lax.dot_general(
            cot[TOK:, :], wb[r, start:ROWS, :], transposed, preferred_element_type=F32
        ).astype(BF16)
        ig_sent(r).start()
        ig_ref[0, :, own_columns(r, 0, ROWS)] = lax.dot_general(
            cot[:TOK, :], wb[r, :ROWS, :], transposed, preferred_element_type=F32
        ).astype(BF16)
        if r != 4:
            ig_ref[0, :, pair_columns(r, 0, PURE)] = lax.dot_general(
                cot[:TOK, :], wb[r, ROWS:, :], transposed, preferred_element_type=F32
            ).astype(BF16)

    def pass_on(r, i):
        for d in (UP, DOWN):
            c = 2 if i == 2 else (first[d] if i == 0 else 1 - first[d])
            gather(d, r, c).wait_recv()
            if r + 1 < 3:
                gather(d, r + 1, c).start()
            elif i == 0:
                fourth_start(d, 0)
                fourth_start(d, 1)
            elif i == 1:
                fourth_start(d, 2)

    pl.semaphore_wait(
        barrier, 1 + count(z > 0) + count(z == Z - 1) + count(yl == 1) + count(isl != ROOT)
    )
    pl.when(yl == 1)(lambda: greet(pair_in, pair))
    pl.when(z > 0)(lambda: greet(above, down))
    pl.when(z == Z - 1)(lambda: greet(below, up))

    def start_gather(d):
        gather(d, 0, first[d]).start()
        gather(d, 0, 1 - first[d]).start()

    pl.when(yl == 0)(lambda: pl.semaphore_wait(pair_in, 1))
    y_w.start()
    y_c.start()
    pl.when(z > 0)(lambda: start_gather(DOWN))
    for s in (4, 3, 5, 2):
        y_x[s].start()
    pl.when(z < Z - 1)(lambda: pl.semaphore_wait(above, 1))
    start_gather(UP)
    pl.when(isl != ROOT)(lambda: greet(here, (ROOT, fs)))
    for copy in local:
        copy.start()
    for s in (4, 3, 5, 2, 6, 1, 7, 0):
        own_x[s].start()

    @pl.when(z == 0)
    def _():
        pl.semaphore_wait(below, 1)
        start_gather(DOWN)

    @pl.when(isl == ROOT)
    def _():
        pl.semaphore_wait(here, ISLANDS - 1)
        for j in range(1, ISLANDS):
            greet(all_in, (lax.rem(isl + j, ISLANDS), fs))

    @pl.when(isl != ROOT)
    def _():
        pl.semaphore_wait(all_in, 1)

    for copy in c_1:
        copy.start()
    y_w.wait_recv()
    for d in (UP, DOWN):
        gather(d, 0, 2).start()
    pass_on(0, 0)
    for copy in local[:3]:
        copy.wait()
    total = pg_own[...].astype(F32)
    for j in range(1, PLANE):
        c_1[j - 1].wait_recv()
        total = total + c_in[j - 1].astype(F32)
    c_out[...] = total.astype(BF16)
    c_2.start()
    for s in (6, 1, 7, 0):
        y_x[s].start()
    y_c.wait_recv()
    make_ig(0)
    pass_on(0, 1)
    pass_on(0, 2)
    make_term(4)
    make_ig(1)
    make_ig(7)
    pass_on(1, 0)
    make_term(3)
    pass_on(1, 1)
    make_term(5)
    pass_on(1, 2)
    make_ig(2)
    make_ig(6)
    make_term(2)
    pass_on(2, 0)
    c_2.wait_recv()
    avg[own_piece, :] = (c_out[...].astype(F32) + c_far[...].astype(F32)) * (1.0 / 16)
    for copy in c_3:
        copy.start()
    make_term(6)
    pass_on(2, 1)
    pass_on(2, 2)
    for d in (UP, DOWN):
        send_sum(d, 4, half_of[d][0], False)
    for d in (UP, DOWN):
        send_sum(d, 3, half_of[d][1], False)
    make_ig(3)
    make_ig(5)
    make_term(1)
    for d in (UP, DOWN):
        for c in range(3):
            only(last_hop[d][c][3], fourth(d, c).wait_recv)
    make_ig(4)
    make_term(7)
    for d in (UP, DOWN):
        send_sum(d, 3, half_of[d][0], True)
    make_term(0)
    for h in (1, 0):
        for d in (UP, DOWN):
            send_sum(d, 2, half_of[d][h], True)

    for copy in local[3:]:
        copy.wait()
    for j in range(1, PLANE):
        c_3_arrival(j).wait_recv()

    @pl.loop(0, ROWS // 64)
    def _(i):
        part = pl.ds(pl.multiple_of(i * 64, 64), 64)
        average = avg[part, :]
        momentum = outer_beta * omb[part, :] + average
        nm_ref[part, :] = momentum
        np_ref[part, :] = opb[part, :] - outer_rate * (average + outer_beta * momentum)

    for h in (1, 0):
        for d in (UP, DOWN):
            send_sum(d, 1, half_of[d][h], True)

    y_w.wait_send()
    y_c.wait_send()
    c_2.wait_send()
    for s in range(Z):
        y_x[s].wait_send()
    for j in range(1, PLANE):
        c_1[j - 1].wait_send()
        c_3[j - 1].wait_send()
    for d in (UP, DOWN):
        for r in range(3):
            for c in range(3):
                gather(d, r, c).wait_send()
        for c in range(3):
            only(last_hop[d][c][2], fourth(d, c).wait_send)
        reduce_copy(d, 4, half_of[d][0]).wait_send()
        for k in (3, 2):
            for h in (0, 1):
                reduce_copy(d, k, h).wait_send()
    for r in (0, 1, 7, 2, 6):
        ig_sent(r).wait_send()
        ig_arrival(r).wait_recv()

    for last in (False, True):
        for d in (UP, DOWN):
            h = half_of[d][0 if last else 1]
            reduce_copy(d, 1, h).wait_recv()
            part = rows(h * HALF, HALF)
            arrived = rs_in[d, 0, part, :].astype(F32)
            if last:
                wg_ref[0, part, :] = (wg_ref[0, part, :] + arrived) * (1.0 / 4096)
            else:
                wg_ref[0, part, :] = term[0, part, :] + arrived

    for d in (UP, DOWN):
        for h in (0, 1):
            reduce_copy(d, 1, h).wait_send()
    for r in (3, 5, 4):
        ig_sent(r).wait_send()
        ig_arrival(r).wait_recv()


def finish_kernel(a, b, c, d, a_out, b_out, c_out, d_out, sems):
    copies = [pltpu.make_async_copy(x, y, sems.at[n]) for n, (x, y) in enumerate(
        [(a, a_out), (b, b_out), (c, c_out), (d, d_out)])]
    for copy in copies:
        copy.start()
    for copy in copies:
        copy.wait()


def finish(*arrays):
    return pl.pallas_call(
        finish_kernel,
        name="finish",
        out_shape=tuple(jax.ShapeDtypeStruct(x.shape, x.dtype) for x in arrays),
        in_specs=[pl.BlockSpec(memory_space=pltpu.VMEM)] * 4,
        out_specs=(pl.BlockSpec(memory_space=pltpu.HBM),) * 4,
        scratch_shapes=[pltpu.SemaphoreType.DMA((4,))],
        compiler_params=pltpu.CompilerParams(vmem_limit_bytes=2**20),
    )(*[pltpu.with_memory_space_constraint(x, pltpu.VMEM) for x in arrays])


def body(inputs, cotangent, key_weight, pseudo_grads, outer_params, outer_momentum):
    dma = pltpu.SemaphoreType.DMA
    vmem = pltpu.VMEM
    anywhere = pl.BlockSpec(memory_space=pltpu.HBM)
    return finish(*pl.pallas_call(
        kernel,
        name="key_backward",
        out_shape=(
            vmem((1, TOK, 2 * Z * ROWS), BF16),
            vmem((1, ROWS, KW), F32),
            vmem((ROWS, KW), F32),
            vmem((ROWS, KW), F32),
        ),
        in_specs=[anywhere] * 6,
        out_specs=(pl.BlockSpec(memory_space=vmem),) * 4,
        scratch_shapes=[
            vmem((2 * TOK, KW), BF16),
            vmem((Z, 2 * TOK, ROWS), BF16),
            vmem((Z, ROWS + PURE, KW), BF16),
            vmem((Z, ROWS, KW), F32),
            vmem((2, 4, ROWS, KW), BF16),
            vmem((2, 4, ROWS, KW), BF16),
            vmem((Z, TOK, HYB), BF16),
            vmem((TOK, ROWS), BF16),
            vmem((PIECE, KW), BF16),
            vmem((PLANE - 1, PIECE, KW), BF16),
            vmem((PIECE, KW), BF16),
            vmem((PIECE, KW), BF16),
            vmem((ROWS, KW), F32),
            vmem((ROWS, KW), F32),
            vmem((ROWS, KW), F32),
            dma((2, 4, 3)), dma((2, 4, 3)),
            dma((2, 4, 2)), dma((2, 4, 2)),
            dma((Z,)), dma((Z,)),
            dma, dma, dma, dma,
            dma((Z,)), dma((Z,)),
            dma((PLANE - 1,)), dma((PLANE - 1,)),
            dma, dma,
            dma((PLANE - 1,)), dma((PLANE - 1,)),
            dma((Z,)), dma((5,)),
        ]
        + [pltpu.SemaphoreType.REGULAR] * 5,
        compiler_params=pltpu.CompilerParams(
            collective_id=0, has_side_effects=True, vmem_limit_bytes=54 * 2**20
        ),
        cost_estimate=pl.CostEstimate(
            flops=4 * TOK * 2 * Z * ROWS * KW, bytes_accessed=24 * 2**20, transcendentals=0
        ),
    )(inputs, cotangent, key_weight, pseudo_grads, outer_params, outer_momentum))


def solution(mesh):
    return jax.shard_map(
        body,
        mesh=mesh,
        in_specs=(
            P("island", "fsdp", None),
            P("island", "fsdp", None),
            P("island", "fsdp", None),
            P("island", "fsdp", None),
            P("fsdp", None),
            P("fsdp", None),
        ),
        out_specs=(
            P("island", "fsdp", None),
            P("island", "fsdp", None),
            P("fsdp", None),
            P("fsdp", None),
        ),
        check_vma=False,
    )
```

```python
import functools

import jax
import jax.numpy as jnp
from jax import lax
from jax.experimental import pallas as pl
from jax.experimental.pallas import tpu as pltpu
from jax.sharding import PartitionSpec as P

outer_rate = 0.7
outer_beta = 0.9

MESH = pl.DeviceIdType.MESH
F32 = jnp.float32
BF16 = jnp.bfloat16

Z = 8
PLANE = 8
ROWS = 512
HALF = ROWS // 2
TOK = 256
PURE = 128
KW = 512
PIECE = ROWS // PLANE

UP, DOWN = 0, 1
ISLANDS = 2 * PLANE
SIDE = 96
ROOT = 1


def rows(start, size):
    return pl.ds(start, size)


def kernel(
    x_ref, c_ref, w_ref, pg_ref, op_ref, om_ref,
    ig_ref, wg_ref, np_ref, nm_ref,
    cot, xin, wb, term, rs_in, rs_out, ig_far,
    pg_own, c_in, c_out, c_far, avg, opb, omb,
    y_s, ag_s, ag4_s, rs_s, c1_s, c3_s,
    ag_r, rs_r, yx_r, yc_r, yw_r, yi_r, c1_r, c2_r, c3_r,
    lx, lm, above, below, pair_in, here, all_in,
):
    isl = lax.axis_index("island")
    fs = lax.axis_index("fsdp")
    z, yl = lax.rem(fs, Z), fs // Z
    q, yh = lax.rem(isl, PLANE), isl // PLANE
    up = (isl, yl * Z + lax.rem(z + 1, Z))
    down = (isl, yl * Z + lax.rem(z + Z - 1, Z))
    pair = (isl, (1 - yl) * Z + z)
    far = ((1 - yh) * PLANE + q, fs)
    plane = [(yh * PLANE + lax.rem(q + j, PLANE), fs) for j in range(1, PLANE)]
    ring = (up, down)

    barrier = pltpu.get_barrier_semaphore()
    def greet(sem, peer):
        pl.semaphore_signal(sem, inc=1, device_id=peer, device_id_type=MESH)

    pl.when(yl == 0)(lambda: greet(barrier, pair))
    greet(barrier, (isl, fs))
    pl.when(z < Z - 1)(lambda: greet(barrier, up))
    pl.when(z == 0)(lambda: greet(barrier, down))

    root = (yh * PLANE + ROOT, fs)
    low_root = isl == ROOT
    high_root = isl == PLANE + ROOT

    @pl.when(q == ROOT)
    def _():
        for peer in plane:
            greet(barrier, peer)
        pl.when(yh == 0)(lambda: greet(barrier, far))

    def count(condition):
        return jnp.where(condition, 1, 0)

    def remote(src, dst, ss, rs, peer):
        return pltpu.make_async_remote_copy(
            src_ref=src, dst_ref=dst, send_sem=ss, recv_sem=rs, device_id=peer, device_id_type=MESH
        )

    def columns(owner_yl, s):
        return pl.ds(pl.multiple_of((owner_yl * Z + lax.rem(z + s, Z)) * ROWS, ROWS), ROWS)

    local = [
        pltpu.make_async_copy(c_ref.at[0], cot.at[rows(0, TOK)], lm),
        pltpu.make_async_copy(w_ref.at[0], wb.at[0, rows(0, ROWS)], lm),
        pltpu.make_async_copy(
            pg_ref.at[0, pl.ds(pl.multiple_of(q * PIECE, PIECE), PIECE)], pg_own, lm
        ),
        pltpu.make_async_copy(op_ref, opb, lm),
        pltpu.make_async_copy(om_ref, omb, lm),
    ]
    own_x = [
        pltpu.make_async_copy(x_ref.at[0, :, columns(yl, s)], xin.at[s, rows(0, TOK)], lx)
        for s in range(Z)
    ]
    y_w = remote(w_ref.at[0, rows(0, PURE)], wb.at[0, rows(ROWS, PURE)], y_s, yw_r, pair)
    y_c = remote(c_ref.at[0], cot.at[rows(TOK, TOK)], y_s, yc_r, pair)
    y_x = [
        remote(x_ref.at[0, :, columns(1 - yl, s)], xin.at[s, rows(TOK, TOK)], y_s, yx_r.at[s], pair)
        for s in range(Z)
    ]

    cuts = {
        0: (0, HALF),
        1: (HALF, HALF),
        2: (ROWS, PURE),
    }

    def slot(d, r):
        return r if d == UP else (Z - r) % Z

    def gather(d, r, c):
        start, size = cuts[c]
        src = w_ref.at[0, rows(start, size)] if r == 0 and c < 2 else wb.at[slot(d, r), rows(start, size)]
        dst = wb.at[slot(d, r + 1), rows(start, size)]
        return remote(src, dst, ag_s, ag_r.at[d, r, c], ring[d])

    first = {UP: 0, DOWN: 1}

    last_hop = {
        UP: (
            (0, HALF - SIDE, None, None),
            (HALF - SIDE, SIDE, z < Z - 1, z > 0),
            (HALF, SIDE, z == Z - 2, z == Z - 1),
        ),
        DOWN: (
            (HALF + SIDE, HALF - SIDE, None, None),
            (HALF, SIDE, z > 0, z < Z - 1),
            (HALF - SIDE, SIDE, z == 1, z == 0),
        ),
    }

    def fourth(d, c):
        start, size = last_hop[d][c][:2]
        return remote(
            wb.at[slot(d, 3), rows(start, size)], wb.at[4, rows(start, size)],
            ag4_s.at[d, c], ag_r.at[d, 3, c], ring[d],
        )

    def only(condition, action):
        if condition is None:
            action()
        else:
            pl.when(condition)(action)

    def fourth_start(d, c):
        only(last_hop[d][c][2], lambda: fourth(d, c).start())

    c_1 = [
        remote(
            pg_ref.at[0, pl.ds(pl.multiple_of(lax.rem(q + j, PLANE) * PIECE, PIECE), PIECE)],
            c_in.at[j - 1], c1_s, c1_r, plane[j - 1],
        )
        for j in range(1, PLANE)
    ]
    c_2 = remote(c_out, c_far, y_s, c2_r, far)
    own_piece = pl.ds(pl.multiple_of(q * PIECE, PIECE), PIECE)
    c_3 = [
        remote(avg.at[own_piece], avg.at[own_piece], c3_s, c3_r, plane[j - 1])
        for j in range(1, PLANE)
    ]

    def bytes_of(kib):
        return ig_ref.at[0, :, pl.ds(0, 2 * kib)]

    def sent(sem, kib):
        remote(bytes_of(kib), bytes_of(kib), sem, sem, pair).wait_send()

    def arrived(sem, kib):
        remote(bytes_of(kib), bytes_of(kib), sem, sem, pair).wait_recv()

    def loaded(sem, kib):
        pltpu.make_async_copy(bytes_of(kib), bytes_of(kib), sem).wait()

    half_of = {UP: (0, 1), DOWN: (1, 0)}

    def reduce_copy(d, k, h):
        part = rows(h * HALF, HALF)
        return remote(
            rs_out.at[d, k - 1, part], rs_in.at[d, k - 1, part],
            rs_s, rs_r.at[d, k - 1, h], ring[d],
        )

    def target(d, k):
        return k if d == UP else Z - k

    def by_rows(start, size, step, action):
        @pl.loop(0, size // step)
        def _(i):
            action(pl.ds(pl.multiple_of(start + i * step, step), step))

    def send_sum(d, k, h, chained):
        if chained:
            reduce_copy(d, k + 1, h).wait_recv()

        def add(part):
            total = term[target(d, k), part, :]
            if chained:
                total = total + rs_in[d, k, part, :].astype(F32)
            rs_out[d, k - 1, part, :] = total.astype(BF16)

        by_rows(h * HALF, HALF, 32, add)
        reduce_copy(d, k, h).start()

    def make_term(s):
        y_x[s].wait_recv()

        @pl.loop(0, ROWS // 128)
        def _(i):
            part = pl.ds(pl.multiple_of(i * 128, 128), 128)
            term[s, part, :] = lax.dot_general(
                xin[s, :, part], cot[...], (((0,), (0,)), ((), ())), preferred_element_type=F32
            )

    def own_columns(r, start, size):
        return pl.ds(pl.multiple_of((yl * Z + lax.rem(z + Z - r, Z)) * ROWS + start, 128), size)

    def pair_columns(r, start, size):
        return pl.ds(pl.multiple_of(((1 - yl) * Z + lax.rem(z + Z - r, Z)) * ROWS + start, 128), size)

    def far_start(r):
        return 0 if r == 4 else PURE

    def ig_sent(r):
        start = far_start(r)
        size = ROWS - start
        return remote(
            ig_far.at[r, :, pl.ds(start, size)], ig_ref.at[0, :, own_columns(r, start, size)],
            y_s, yi_r, pair,
        )

    def make_ig(r):
        transposed = (((1,), (1,)), ((), ()))

        @pl.loop(0, ROWS // 128)
        def _(i):
            start = pl.multiple_of(i * 128, 128)
            product = lax.dot_general(
                cot[...], wb[r, pl.ds(start, 128), :], transposed, preferred_element_type=F32
            ).astype(BF16)
            ig_ref[0, :, own_columns(r, start, 128)] = product[:TOK]
            ig_far[r, :, pl.ds(start, 128)] = product[TOK:]

        ig_sent(r).start()
        if r != 4:
            ig_ref[0, :, pair_columns(r, 0, PURE)] = lax.dot_general(
                cot[:TOK, :], wb[r, ROWS:, :], transposed, preferred_element_type=F32
            ).astype(BF16)

    def pass_on(r, i):
        for d in (UP, DOWN):
            c = 2 if i == 2 else (first[d] if i == 0 else 1 - first[d])
            gather(d, r, c).wait_recv()
            if r + 1 < 3:
                gather(d, r + 1, c).start()
            elif i == 0:
                fourth_start(d, 0)
                fourth_start(d, 1)
            elif i == 1:
                fourth_start(d, 2)

    pl.semaphore_wait(
        barrier, 1 + count(z > 0) + count(z == Z - 1) + count(yl == 1) + count(q != ROOT) + count(high_root)
    )
    pl.when(yl == 1)(lambda: greet(pair_in, pair))
    pl.when(z > 0)(lambda: greet(above, down))
    pl.when(z == Z - 1)(lambda: greet(below, up))

    def start_gather(d):
        gather(d, 0, first[d]).start()
        gather(d, 0, 1 - first[d]).start()

    pl.when(yl == 0)(lambda: pl.semaphore_wait(pair_in, 1))
    y_w.start()
    y_c.start()
    pl.when(z > 0)(lambda: start_gather(DOWN))
    for s in (4, 3, 5, 2):
        y_x[s].start()
    pl.when(z < Z - 1)(lambda: pl.semaphore_wait(above, 1))
    start_gather(UP)
    pl.when(q != ROOT)(lambda: greet(here, root))
    for copy in local:
        copy.start()
    for s in (4, 3, 5, 2, 6, 1, 7, 0):
        own_x[s].start()

    @pl.when(z == 0)
    def _():
        pl.semaphore_wait(below, 1)
        start_gather(DOWN)

    @pl.when(high_root)
    def _():
        pl.semaphore_wait(here, PLANE - 1)
        greet(here, far)

    @pl.when(low_root)
    def _():
        pl.semaphore_wait(here, PLANE)
        for j in range(1, ISLANDS):
            greet(all_in, (lax.rem(isl + j, ISLANDS), fs))

    @pl.when(isl != ROOT)
    def _():
        pl.semaphore_wait(all_in, 1)

    for copy in c_1:
        copy.start()
    y_w.wait_recv()
    for d in (UP, DOWN):
        gather(d, 0, 2).start()
    pass_on(0, 0)
    loaded(lm, 256 + 512 + 64 + 1024 + 1024)
    loaded(lx, 8 * 256)
    arrived(c1_r, 7 * 64)

    def plane_sum(part):
        total = pg_own[part, :].astype(F32)
        for j in range(1, PLANE):
            total = total + c_in[j - 1, part, :].astype(F32)
        c_out[part, :] = total.astype(BF16)

    by_rows(0, PIECE, 16, plane_sum)
    c_2.start()
    for s in (6, 1, 7, 0):
        y_x[s].start()
    y_c.wait_recv()
    make_ig(0)
    pass_on(0, 1)
    pass_on(0, 2)
    make_term(4)
    make_ig(1)
    make_ig(7)
    pass_on(1, 0)
    make_term(3)
    pass_on(1, 1)
    make_term(5)
    pass_on(1, 2)
    make_ig(2)
    make_ig(6)
    make_term(2)
    pass_on(2, 0)
    c_2.wait_recv()
    avg[own_piece, :] = (c_out[...].astype(F32) + c_far[...].astype(F32)) * (1.0 / 16)
    for copy in c_3:
        copy.start()
    make_term(6)
    pass_on(2, 1)
    pass_on(2, 2)
    for d in (UP, DOWN):
        send_sum(d, 4, half_of[d][0], False)
    for d in (UP, DOWN):
        send_sum(d, 3, half_of[d][1], False)
    make_ig(3)
    make_ig(5)
    make_term(1)
    for d in (UP, DOWN):
        for c in range(3):
            only(last_hop[d][c][3], fourth(d, c).wait_recv)
    make_ig(4)
    make_term(7)
    for d in (UP, DOWN):
        send_sum(d, 3, half_of[d][0], True)
    make_term(0)
    for h in (1, 0):
        for d in (UP, DOWN):
            send_sum(d, 2, half_of[d][h], True)

    arrived(c3_r, 7 * 128)

    def update(part):
        average = avg[part, :]
        momentum = outer_beta * omb[part, :] + average
        nm_ref[part, :] = momentum
        np_ref[part, :] = opb[part, :] - outer_rate * (average + outer_beta * momentum)

    by_rows(0, ROWS, 16, update)

    for h in (1, 0):
        for d in (UP, DOWN):
            send_sum(d, 1, half_of[d][h], True)

    sent(c1_s, 7 * 64)
    sent(c3_s, 7 * 128)
    sent(ag_s, 2 * 3 * (ROWS + PURE))
    for d in (UP, DOWN):
        for c in range(3):
            only(last_hop[d][c][2], fourth(d, c).wait_send)

    for last in (False, True):
        for d in (UP, DOWN):
            h = half_of[d][0 if last else 1]
            reduce_copy(d, 1, h).wait_recv()

            def add(part):
                arrived = rs_in[d, 0, part, :].astype(F32)
                if last:
                    wg_ref[0, part, :] = (wg_ref[0, part, :] + arrived) * (1.0 / 4096)
                else:
                    wg_ref[0, part, :] = term[0, part, :] + arrived

            by_rows(h * HALF, HALF, 32, add)

    sent(rs_s, 2 * 7 * HALF)
    sent(y_s, PURE + TOK + 8 * TOK + PIECE + 7 * (TOK * 3 // 4) + TOK)
    arrived(yi_r, 7 * (TOK * 3 // 4) + TOK)


def finish_kernel(a, b, c, d, a_out, b_out, c_out, d_out, sems):
    copies = [pltpu.make_async_copy(x, y, sems.at[n]) for n, (x, y) in enumerate(
        [(a, a_out), (b, b_out), (c, c_out), (d, d_out)])]
    for copy in copies:
        copy.start()
    for copy in copies:
        copy.wait()


def finish(*arrays):
    return pl.pallas_call(
        finish_kernel,
        name="finish",
        out_shape=tuple(jax.ShapeDtypeStruct(x.shape, x.dtype) for x in arrays),
        in_specs=[pl.BlockSpec(memory_space=pltpu.VMEM)] * 4,
        out_specs=(pl.BlockSpec(memory_space=pltpu.HBM),) * 4,
        scratch_shapes=[pltpu.SemaphoreType.DMA((4,))],
        compiler_params=pltpu.CompilerParams(vmem_limit_bytes=2**20),
    )(*[pltpu.with_memory_space_constraint(x, pltpu.VMEM) for x in arrays])


def body(inputs, cotangent, key_weight, pseudo_grads, outer_params, outer_momentum):
    dma = pltpu.SemaphoreType.DMA
    vmem = pltpu.VMEM
    anywhere = pl.BlockSpec(memory_space=pltpu.HBM)
    return finish(*pl.pallas_call(
        kernel,
        name="key_backward",
        out_shape=(
            vmem((1, TOK, 2 * Z * ROWS), BF16),
            vmem((1, ROWS, KW), F32),
            vmem((ROWS, KW), F32),
            vmem((ROWS, KW), F32),
        ),
        in_specs=[anywhere] * 6,
        out_specs=(pl.BlockSpec(memory_space=vmem),) * 4,
        scratch_shapes=[
            vmem((2 * TOK, KW), BF16),
            vmem((Z, 2 * TOK, ROWS), BF16),
            vmem((Z, ROWS + PURE, KW), BF16),
            vmem((Z, ROWS, KW), F32),
            vmem((2, 4, ROWS, KW), BF16),
            vmem((2, 4, ROWS, KW), BF16),
            vmem((Z, TOK, ROWS), BF16),
            vmem((PIECE, KW), BF16),
            vmem((PLANE - 1, PIECE, KW), BF16),
            vmem((PIECE, KW), BF16),
            vmem((PIECE, KW), BF16),
            vmem((ROWS, KW), F32),
            vmem((ROWS, KW), F32),
            vmem((ROWS, KW), F32),
            dma, dma, dma((2, 3)), dma, dma, dma,
            dma((2, 4, 3)), dma((2, 4, 2)), dma((Z,)), dma, dma,
            dma, dma, dma, dma, dma, dma,
        ]
        + [pltpu.SemaphoreType.REGULAR] * 5,
        compiler_params=pltpu.CompilerParams(
            collective_id=0, has_side_effects=True, vmem_limit_bytes=54 * 2**20
        ),
        cost_estimate=pl.CostEstimate(
            flops=4 * TOK * 2 * Z * ROWS * KW, bytes_accessed=24 * 2**20, transcendentals=0
        ),
    )(inputs, cotangent, key_weight, pseudo_grads, outer_params, outer_momentum))


def solution(mesh):
    return jax.shard_map(
        body,
        mesh=mesh,
        in_specs=(
            P("island", "fsdp", None),
            P("island", "fsdp", None),
            P("island", "fsdp", None),
            P("island", "fsdp", None),
            P("fsdp", None),
            P("fsdp", None),
        ),
        out_specs=(
            P("island", "fsdp", None),
            P("island", "fsdp", None),
            P("fsdp", None),
            P("fsdp", None),
        ),
        check_vma=False,
    )
```

```python
import functools

import jax
import jax.numpy as jnp
from jax import lax
from jax.experimental import pallas as pl
from jax.experimental.pallas import tpu as pltpu
from jax.sharding import PartitionSpec as P

outer_rate = 0.7
outer_beta = 0.9

MESH = pl.DeviceIdType.MESH
F32 = jnp.float32
BF16 = jnp.bfloat16

Z = 8
PLANE = 8
ROWS = 512
HALF = ROWS // 2
TOK = 256
PURE = 128
KW = 512
PIECE = ROWS // PLANE

UP, DOWN = 0, 1
ISLANDS = 2 * PLANE
SIDE = 96
ROOT = 1


def rows(start, size):
    return pl.ds(start, size)


def kernel(
    x_ref, c_ref, w_ref, pg_ref, op_ref, om_ref,
    ig_ref, wg_ref, np_ref, nm_ref,
    cot, xin, wb, term, rs_in, rs_out, ig_far,
    pg_own, c_in, c_out, c_far, avg, opb, omb,
    y_s, ag_s, ag4_s, rs_s, c1_s, c3_s,
    ag_r, ag4_r, rs_r, yx_r, yc_r, yw_r, yi_r, c1_r, c2_r, c3_r,
    lx, lm, above, below, here, all_in,
):
    isl = lax.axis_index("island")
    fs = lax.axis_index("fsdp")
    z, yl = lax.rem(fs, Z), fs // Z
    q, yh = lax.rem(isl, PLANE), isl // PLANE
    up = (isl, yl * Z + lax.rem(z + 1, Z))
    down = (isl, yl * Z + lax.rem(z + Z - 1, Z))
    pair = (isl, (1 - yl) * Z + z)
    far = ((1 - yh) * PLANE + q, fs)
    plane = [(yh * PLANE + lax.rem(q + j, PLANE), fs) for j in range(1, PLANE)]
    ring = (up, down)

    barrier = pltpu.get_barrier_semaphore()
    def greet(sem, peer):
        pl.semaphore_signal(sem, inc=1, device_id=peer, device_id_type=MESH)

    greet(barrier, pair)
    greet(barrier, (isl, fs))
    pl.when(z < Z - 1)(lambda: greet(barrier, up))
    pl.when(z == 0)(lambda: greet(barrier, down))

    root = (yh * PLANE + ROOT, fs)
    low_root = isl == ROOT
    high_root = isl == PLANE + ROOT

    @pl.when(q == ROOT)
    def _():
        for peer in plane:
            greet(barrier, peer)
        pl.when(yh == 0)(lambda: greet(barrier, far))

    def count(condition):
        return jnp.where(condition, 1, 0)

    def remote(src, dst, ss, rs, peer):
        return pltpu.make_async_remote_copy(
            src_ref=src, dst_ref=dst, send_sem=ss, recv_sem=rs, device_id=peer, device_id_type=MESH
        )

    def columns(owner_yl, s):
        return pl.ds(pl.multiple_of((owner_yl * Z + lax.rem(z + s, Z)) * ROWS, ROWS), ROWS)

    local = [
        pltpu.make_async_copy(c_ref.at[0], cot.at[rows(0, TOK)], lm),
        pltpu.make_async_copy(w_ref.at[0], wb.at[0, rows(0, ROWS)], lm),
        pltpu.make_async_copy(
            pg_ref.at[0, pl.ds(pl.multiple_of(q * PIECE, PIECE), PIECE)], pg_own, lm
        ),
        pltpu.make_async_copy(op_ref, opb, lm),
        pltpu.make_async_copy(om_ref, omb, lm),
    ]
    own_x = [
        pltpu.make_async_copy(x_ref.at[0, :, columns(yl, s)], xin.at[s, rows(0, TOK)], lx)
        for s in range(Z)
    ]
    y_w = remote(w_ref.at[0, rows(0, PURE)], wb.at[0, rows(ROWS, PURE)], y_s, yw_r, pair)
    y_c = remote(c_ref.at[0], cot.at[rows(TOK, TOK)], y_s, yc_r, pair)
    y_x = [
        remote(x_ref.at[0, :, columns(1 - yl, s)], xin.at[s, rows(TOK, TOK)], y_s, yx_r.at[s], pair)
        for s in range(Z)
    ]

    cuts = {
        0: (0, HALF),
        1: (HALF, HALF),
        2: (ROWS, PURE),
    }

    def slot(d, r):
        return r if d == UP else (Z - r) % Z

    def gather(d, r, c):
        start, size = cuts[c]
        src = w_ref.at[0, rows(start, size)] if r == 0 and c < 2 else wb.at[slot(d, r), rows(start, size)]
        dst = wb.at[slot(d, r + 1), rows(start, size)]
        return remote(src, dst, ag_s, ag_r.at[d, r, 0 if c == first[d] else 1], ring[d])

    first = {UP: 0, DOWN: 1}

    last_hop = {
        UP: (
            (0, HALF - SIDE, None),
            (HALF - SIDE, SIDE, z < Z - 1),
            (HALF, SIDE, z == Z - 2),
        ),
        DOWN: (
            (HALF + SIDE, HALF - SIDE, None),
            (HALF, SIDE, z > 0),
            (HALF - SIDE, SIDE, z == 1),
        ),
    }

    def fourth(d, c):
        start, size = last_hop[d][c][:2]
        return remote(
            wb.at[slot(d, 3), rows(start, size)], wb.at[4, rows(start, size)],
            ag4_s, ag4_r, ring[d],
        )

    def only(condition, action):
        if condition is None:
            action()
        else:
            pl.when(condition)(action)

    def fourth_start(d, c):
        only(last_hop[d][c][2], lambda: fourth(d, c).start())

    c_1 = [
        remote(
            pg_ref.at[0, pl.ds(pl.multiple_of(lax.rem(q + j, PLANE) * PIECE, PIECE), PIECE)],
            c_in.at[j - 1], c1_s, c1_r, plane[j - 1],
        )
        for j in range(1, PLANE)
    ]
    c_2 = remote(c_out, c_far, y_s, c2_r, far)
    own_piece = pl.ds(pl.multiple_of(q * PIECE, PIECE), PIECE)
    c_3 = [
        remote(avg.at[own_piece], avg.at[own_piece], c3_s, c3_r, plane[j - 1])
        for j in range(1, PLANE)
    ]

    def bytes_of(kib):
        return ig_ref.at[0, :, pl.ds(0, 2 * kib)]

    def sent(sem, kib):
        remote(bytes_of(kib), bytes_of(kib), sem, sem, pair).wait_send()

    def arrived(sem, kib):
        remote(bytes_of(kib), bytes_of(kib), sem, sem, pair).wait_recv()

    def loaded(sem, kib):
        pltpu.make_async_copy(bytes_of(kib), bytes_of(kib), sem).wait()

    half_of = {UP: (0, 1), DOWN: (1, 0)}

    def reduce_copy(d, k, h):
        part = rows(h * HALF, HALF)
        return remote(
            rs_out.at[d, k - 1, part], rs_in.at[d, k - 1, part],
            rs_s, rs_r.at[d, 6 if k == 4 else 2 * (k - 1) + h], ring[d],
        )

    def target(d, k):
        return k if d == UP else Z - k

    def by_rows(start, size, step, action):
        @pl.loop(0, size // step)
        def _(i):
            action(pl.ds(pl.multiple_of(start + i * step, step), step))

    def send_sum(d, k, h, chained):
        if chained:
            reduce_copy(d, k + 1, h).wait_recv()

        def add(part):
            total = term[target(d, k), part, :]
            if chained:
                total = total + rs_in[d, k, part, :].astype(F32)
            rs_out[d, k - 1, part, :] = total.astype(BF16)

        by_rows(h * HALF, HALF, 32, add)
        reduce_copy(d, k, h).start()

    def make_term(s):
        y_x[s].wait_recv()

        @pl.loop(0, ROWS // 128)
        def _(i):
            part = pl.ds(pl.multiple_of(i * 128, 128), 128)
            term[s, part, :] = lax.dot_general(
                xin[s, :, part], cot[...], (((0,), (0,)), ((), ())), preferred_element_type=F32
            )

    def own_columns(r, start, size):
        return pl.ds(pl.multiple_of((yl * Z + lax.rem(z + Z - r, Z)) * ROWS + start, 128), size)

    def pair_columns(r, start, size):
        return pl.ds(pl.multiple_of(((1 - yl) * Z + lax.rem(z + Z - r, Z)) * ROWS + start, 128), size)

    def far_start(r):
        return 0 if r == 4 else PURE

    def ig_sent(r):
        start = far_start(r)
        size = ROWS - start
        return remote(
            ig_far.at[r, :, pl.ds(start, size)], ig_ref.at[0, :, own_columns(r, start, size)],
            y_s, yi_r, pair,
        )

    def make_ig(r):
        transposed = (((1,), (1,)), ((), ()))

        @pl.loop(0, ROWS // 128)
        def _(i):
            start = pl.multiple_of(i * 128, 128)
            product = lax.dot_general(
                cot[...], wb[r, pl.ds(start, 128), :], transposed, preferred_element_type=F32
            ).astype(BF16)
            ig_ref[0, :, own_columns(r, start, 128)] = product[:TOK]
            ig_far[r, :, pl.ds(start, 128)] = product[TOK:]

        ig_sent(r).start()
        if r != 4:
            ig_ref[0, :, pair_columns(r, 0, PURE)] = lax.dot_general(
                cot[:TOK, :], wb[r, ROWS:, :], transposed, preferred_element_type=F32
            ).astype(BF16)

    def pass_on(r, i):
        for d in (UP, DOWN):
            if i == 0:
                gather(d, r, first[d]).wait_recv()
            else:
                arrived(ag_r.at[d, r, 1], HALF + PURE)
            if r + 1 < 3:
                for c in (first[d],) if i == 0 else (1 - first[d], 2):
                    gather(d, r + 1, c).start()
            else:
                for c in (0, 1) if i == 0 else (2,):
                    fourth_start(d, c)

    pl.semaphore_wait(
        barrier, 2 + count(z > 0) + count(z == Z - 1) + count(q != ROOT) + count(high_root)
    )
    pl.when(z > 0)(lambda: greet(above, down))
    pl.when(z == Z - 1)(lambda: greet(below, up))

    def start_gather(d):
        gather(d, 0, first[d]).start()
        gather(d, 0, 1 - first[d]).start()

    y_w.start()
    y_c.start()
    pl.when(z > 0)(lambda: start_gather(DOWN))
    for s in (4, 3, 5, 2):
        y_x[s].start()
    pl.when(z < Z - 1)(lambda: pl.semaphore_wait(above, 1))
    start_gather(UP)
    pl.when(q != ROOT)(lambda: greet(here, root))
    for copy in local:
        copy.start()
    for s in (4, 3, 5, 2, 6, 1, 7, 0):
        own_x[s].start()

    @pl.when(z == 0)
    def _():
        pl.semaphore_wait(below, 1)
        start_gather(DOWN)

    @pl.when(high_root)
    def _():
        pl.semaphore_wait(here, PLANE - 1)
        greet(here, far)

    @pl.when(low_root)
    def _():
        pl.semaphore_wait(here, PLANE)
        for j in range(1, ISLANDS):
            greet(all_in, (lax.rem(isl + j, ISLANDS), fs))

    @pl.when(isl != ROOT)
    def _():
        pl.semaphore_wait(all_in, 1)

    for copy in c_1:
        copy.start()
    y_w.wait_recv()
    for d in (UP, DOWN):
        gather(d, 0, 2).start()
    pass_on(0, 0)
    loaded(lm, 256 + 512 + 64 + 1024 + 1024)
    loaded(lx, 8 * 256)
    arrived(c1_r, 7 * 64)

    def plane_sum(part):
        total = pg_own[part, :].astype(F32)
        for j in range(1, PLANE):
            total = total + c_in[j - 1, part, :].astype(F32)
        c_out[part, :] = total.astype(BF16)

    by_rows(0, PIECE, 16, plane_sum)
    c_2.start()
    for s in (6, 1, 7, 0):
        y_x[s].start()
    y_c.wait_recv()
    make_ig(0)
    pass_on(0, 1)
    make_term(4)
    make_ig(1)
    make_ig(7)
    pass_on(1, 0)
    make_term(3)
    make_term(5)
    pass_on(1, 1)
    make_ig(2)
    make_ig(6)
    make_term(2)
    pass_on(2, 0)
    c_2.wait_recv()
    avg[own_piece, :] = (c_out[...].astype(F32) + c_far[...].astype(F32)) * (1.0 / 16)
    for copy in c_3:
        copy.start()
    make_term(6)
    pass_on(2, 1)
    for d in (UP, DOWN):
        send_sum(d, 4, half_of[d][0], False)
    for d in (UP, DOWN):
        send_sum(d, 3, half_of[d][1], False)
    make_ig(3)
    make_ig(5)
    make_term(1)
    arrived(ag4_r, ROWS)
    make_ig(4)
    make_term(7)
    for d in (UP, DOWN):
        send_sum(d, 3, half_of[d][0], True)
    make_term(0)
    for h in (1, 0):
        for d in (UP, DOWN):
            send_sum(d, 2, half_of[d][h], True)

    arrived(c3_r, 7 * 128)

    def update(part):
        average = avg[part, :]
        momentum = outer_beta * omb[part, :] + average
        nm_ref[part, :] = momentum
        np_ref[part, :] = opb[part, :] - outer_rate * (average + outer_beta * momentum)

    by_rows(0, ROWS, 16, update)

    for h in (1, 0):
        for d in (UP, DOWN):
            send_sum(d, 1, half_of[d][h], True)

    sent(c1_s, 7 * 64)
    sent(c3_s, 7 * 128)
    sent(ag_s, 2 * 3 * (ROWS + PURE))
    def fourth_sent(size):
        part = wb.at[0, rows(0, size)]
        remote(part, part, ag4_s, ag4_s, pair).wait_send()

    less = (z == 0) | (z == Z - 1)
    more = (z == 1) | (z == Z - 2)
    pl.when(less)(lambda: fourth_sent(ROWS - SIDE))
    pl.when(more)(lambda: fourth_sent(ROWS + SIDE))
    pl.when(jnp.logical_not(less | more))(lambda: fourth_sent(ROWS))

    for last in (False, True):
        for d in (UP, DOWN):
            h = half_of[d][0 if last else 1]
            reduce_copy(d, 1, h).wait_recv()

            def add(part):
                arrived = rs_in[d, 0, part, :].astype(F32)
                if last:
                    wg_ref[0, part, :] = (wg_ref[0, part, :] + arrived) * (1.0 / 4096)
                else:
                    wg_ref[0, part, :] = term[0, part, :] + arrived

            by_rows(h * HALF, HALF, 32, add)

    sent(rs_s, 2 * 7 * HALF)
    sent(y_s, PURE + TOK + 8 * TOK + PIECE + 7 * (TOK * 3 // 4) + TOK)
    arrived(yi_r, 7 * (TOK * 3 // 4) + TOK)


def finish_kernel(a, b, c, d, a_out, b_out, c_out, d_out, sems):
    copies = [pltpu.make_async_copy(x, y, sems.at[n]) for n, (x, y) in enumerate(
        [(a, a_out), (b, b_out), (c, c_out), (d, d_out)])]
    for copy in copies:
        copy.start()
    for copy in copies:
        copy.wait()


def finish(*arrays):
    return pl.pallas_call(
        finish_kernel,
        name="finish",
        out_shape=tuple(jax.ShapeDtypeStruct(x.shape, x.dtype) for x in arrays),
        in_specs=[pl.BlockSpec(memory_space=pltpu.VMEM)] * 4,
        out_specs=(pl.BlockSpec(memory_space=pltpu.HBM),) * 4,
        scratch_shapes=[pltpu.SemaphoreType.DMA((4,))],
        compiler_params=pltpu.CompilerParams(vmem_limit_bytes=2**20),
    )(*[pltpu.with_memory_space_constraint(x, pltpu.VMEM) for x in arrays])


def body(inputs, cotangent, key_weight, pseudo_grads, outer_params, outer_momentum):
    dma = pltpu.SemaphoreType.DMA
    vmem = pltpu.VMEM
    anywhere = pl.BlockSpec(memory_space=pltpu.HBM)
    return finish(*pl.pallas_call(
        kernel,
        name="key_backward",
        out_shape=(
            vmem((1, TOK, 2 * Z * ROWS), BF16),
            vmem((1, ROWS, KW), F32),
            vmem((ROWS, KW), F32),
            vmem((ROWS, KW), F32),
        ),
        in_specs=[anywhere] * 6,
        out_specs=(pl.BlockSpec(memory_space=vmem),) * 4,
        scratch_shapes=[
            vmem((2 * TOK, KW), BF16),
            vmem((Z, 2 * TOK, ROWS), BF16),
            vmem((Z, ROWS + PURE, KW), BF16),
            vmem((Z, ROWS, KW), F32),
            vmem((2, 4, ROWS, KW), BF16),
            vmem((2, 4, ROWS, KW), BF16),
            vmem((Z, TOK, ROWS), BF16),
            vmem((PIECE, KW), BF16),
            vmem((PLANE - 1, PIECE, KW), BF16),
            vmem((PIECE, KW), BF16),
            vmem((PIECE, KW), BF16),
            vmem((ROWS, KW), F32),
            vmem((ROWS, KW), F32),
            vmem((ROWS, KW), F32),
            dma, dma, dma, dma, dma, dma,
            dma((2, 3, 2)), dma, dma((2, 7)), dma((Z,)), dma, dma,
            dma, dma, dma, dma, dma, dma,
        ]
        + [pltpu.SemaphoreType.REGULAR] * 4,
        compiler_params=pltpu.CompilerParams(
            collective_id=0, has_side_effects=True, vmem_limit_bytes=54 * 2**20
        ),
        cost_estimate=pl.CostEstimate(
            flops=4 * TOK * 2 * Z * ROWS * KW, bytes_accessed=24 * 2**20, transcendentals=0
        ),
    )(inputs, cotangent, key_weight, pseudo_grads, outer_params, outer_momentum))


def solution(mesh):
    return jax.shard_map(
        body,
        mesh=mesh,
        in_specs=(
            P("island", "fsdp", None),
            P("island", "fsdp", None),
            P("island", "fsdp", None),
            P("island", "fsdp", None),
            P("fsdp", None),
            P("fsdp", None),
        ),
        out_specs=(
            P("island", "fsdp", None),
            P("island", "fsdp", None),
            P("fsdp", None),
            P("fsdp", None),
        ),
        check_vma=False,
    )
```

```python
import functools

import jax
import jax.numpy as jnp
from jax import lax
from jax.experimental import pallas as pl
from jax.experimental.pallas import tpu as pltpu
from jax.sharding import PartitionSpec as P

outer_rate = 0.7
outer_beta = 0.9

MESH = pl.DeviceIdType.MESH
F32 = jnp.float32
BF16 = jnp.bfloat16

Z = 8
PLANE = 8
ROWS = 512
HALF = ROWS // 2
TOK = 256
PURE = 128
KW = 512
PIECE = ROWS // PLANE

UP, DOWN = 0, 1
ISLANDS = 2 * PLANE
SIDE = 80
ROOT = 1


def rows(start, size):
    return pl.ds(start, size)


def kernel(
    x_ref, c_ref, w_ref, pg_ref, op_ref, om_ref,
    ig_ref, wg_ref, np_ref, nm_ref,
    cot, xin, wb, term, rs_in, rs_out, ig_far,
    pg_own, c_in, c_out, c_far, avg, opb, omb,
    y_s, ag_s, ag4_s, rs_s, c1_s, c3_s,
    ag_r, ag4_r, rs_r, yx_r, yc_r, yw_r, yi_r, c1_r, c2_r, c3_r,
    lx, lm, above, below, here, all_in,
):
    isl = lax.axis_index("island")
    fs = lax.axis_index("fsdp")
    z, yl = lax.rem(fs, Z), fs // Z
    q, yh = lax.rem(isl, PLANE), isl // PLANE
    up = (isl, yl * Z + lax.rem(z + 1, Z))
    down = (isl, yl * Z + lax.rem(z + Z - 1, Z))
    pair = (isl, (1 - yl) * Z + z)
    far = ((1 - yh) * PLANE + q, fs)
    plane = [(yh * PLANE + lax.rem(q + j, PLANE), fs) for j in range(1, PLANE)]
    ring = (up, down)

    barrier = pltpu.get_barrier_semaphore()
    def greet(sem, peer):
        pl.semaphore_signal(sem, inc=1, device_id=peer, device_id_type=MESH)

    greet(barrier, pair)
    greet(barrier, (isl, fs))
    pl.when(z < Z - 1)(lambda: greet(barrier, up))
    pl.when(z == 0)(lambda: greet(barrier, down))

    root = (yh * PLANE + ROOT, fs)
    low_root = isl == ROOT
    high_root = isl == PLANE + ROOT

    @pl.when(q == ROOT)
    def _():
        for peer in plane:
            greet(barrier, peer)
        pl.when(yh == 0)(lambda: greet(barrier, far))

    def count(condition):
        return jnp.where(condition, 1, 0)

    def remote(src, dst, ss, rs, peer):
        return pltpu.make_async_remote_copy(
            src_ref=src, dst_ref=dst, send_sem=ss, recv_sem=rs, device_id=peer, device_id_type=MESH
        )

    def columns(owner_yl, s):
        return pl.ds(pl.multiple_of((owner_yl * Z + lax.rem(z + s, Z)) * ROWS, ROWS), ROWS)

    local = [
        pltpu.make_async_copy(c_ref.at[0], cot.at[rows(0, TOK)], lm),
        pltpu.make_async_copy(w_ref.at[0], wb.at[0, rows(0, ROWS)], lm),
        pltpu.make_async_copy(
            pg_ref.at[0, pl.ds(pl.multiple_of(q * PIECE, PIECE), PIECE)], pg_own, lm
        ),
        pltpu.make_async_copy(op_ref, opb, lm),
        pltpu.make_async_copy(om_ref, omb, lm),
    ]
    own_x = [
        pltpu.make_async_copy(x_ref.at[0, :, columns(yl, s)], xin.at[s, rows(0, TOK)], lx)
        for s in range(Z)
    ]
    y_w = remote(w_ref.at[0, rows(0, PURE)], wb.at[0, rows(ROWS, PURE)], y_s, yw_r, pair)
    y_c = remote(c_ref.at[0], cot.at[rows(TOK, TOK)], y_s, yc_r, pair)
    y_x = [
        remote(x_ref.at[0, :, columns(1 - yl, s)], xin.at[s, rows(TOK, TOK)], y_s, yx_r.at[s], pair)
        for s in range(Z)
    ]

    cuts = {
        0: (0, HALF),
        1: (HALF, HALF),
        2: (ROWS, PURE),
    }

    def slot(d, r):
        return r if d == UP else (Z - r) % Z

    def gather(d, r, c):
        start, size = cuts[c]
        src = w_ref.at[0, rows(start, size)] if r == 0 and c < 2 else wb.at[slot(d, r), rows(start, size)]
        dst = wb.at[slot(d, r + 1), rows(start, size)]
        return remote(src, dst, ag_s, ag_r.at[d, r, 0 if c == first[d] else 1], ring[d])

    first = {UP: 0, DOWN: 1}

    last_hop = {
        UP: (
            (0, HALF - SIDE, None),
            (HALF - SIDE, SIDE, z < Z - 1),
            (HALF, SIDE, z == Z - 2),
        ),
        DOWN: (
            (HALF + SIDE, HALF - SIDE, None),
            (HALF, SIDE, z > 0),
            (HALF - SIDE, SIDE, z == 1),
        ),
    }

    def fourth(d, c):
        start, size = last_hop[d][c][:2]
        return remote(
            wb.at[slot(d, 3), rows(start, size)], wb.at[4, rows(start, size)],
            ag4_s, ag4_r, ring[d],
        )

    def only(condition, action):
        if condition is None:
            action()
        else:
            pl.when(condition)(action)

    def fourth_start(d, c):
        only(last_hop[d][c][2], lambda: fourth(d, c).start())

    c_1 = [
        remote(
            pg_ref.at[0, pl.ds(pl.multiple_of(lax.rem(q + j, PLANE) * PIECE, PIECE), PIECE)],
            c_in.at[j - 1], c1_s, c1_r, plane[j - 1],
        )
        for j in range(1, PLANE)
    ]
    c_2 = remote(c_out, c_far, y_s, c2_r, far)
    own_piece = pl.ds(pl.multiple_of(q * PIECE, PIECE), PIECE)
    c_3 = [
        remote(avg.at[own_piece], avg.at[own_piece], c3_s, c3_r, plane[j - 1])
        for j in range(1, PLANE)
    ]

    def bytes_of(kib):
        return ig_ref.at[0, :, pl.ds(0, 2 * kib)]

    def sent(sem, kib):
        remote(bytes_of(kib), bytes_of(kib), sem, sem, pair).wait_send()

    def arrived(sem, kib):
        remote(bytes_of(kib), bytes_of(kib), sem, sem, pair).wait_recv()

    def loaded(sem, kib):
        pltpu.make_async_copy(bytes_of(kib), bytes_of(kib), sem).wait()

    half_of = {UP: (0, 1), DOWN: (1, 0)}

    def reduce_copy(d, k, h):
        part = rows(h * HALF, HALF)
        return remote(
            rs_out.at[d, k - 1, part], rs_in.at[d, k - 1, part],
            rs_s, rs_r.at[d, 6 if k == 4 else 2 * (k - 1) + h], ring[d],
        )

    def target(d, k):
        return k if d == UP else Z - k

    def by_rows(start, size, step, action):
        @pl.loop(0, size // step)
        def _(i):
            action(pl.ds(pl.multiple_of(start + i * step, step), step))

    def send_sum(d, k, h, chained):
        if chained:
            reduce_copy(d, k + 1, h).wait_recv()

        def add(part):
            total = term[target(d, k), part, :]
            if chained:
                total = total + rs_in[d, k, part, :].astype(F32)
            rs_out[d, k - 1, part, :] = total.astype(BF16)

        by_rows(h * HALF, HALF, 32, add)
        reduce_copy(d, k, h).start()

    def make_term(s):
        y_x[s].wait_recv()

        @pl.loop(0, ROWS // 128)
        def _(i):
            part = pl.ds(pl.multiple_of(i * 128, 128), 128)
            term[s, part, :] = lax.dot_general(
                xin[s, :, part], cot[...], (((0,), (0,)), ((), ())), preferred_element_type=F32
            )

    def own_columns(r, start, size):
        return pl.ds(pl.multiple_of((yl * Z + lax.rem(z + Z - r, Z)) * ROWS + start, 128), size)

    def pair_columns(r, start, size):
        return pl.ds(pl.multiple_of(((1 - yl) * Z + lax.rem(z + Z - r, Z)) * ROWS + start, 128), size)

    def far_start(r):
        return 0 if r == 4 else PURE

    def ig_sent(r):
        start = far_start(r)
        size = ROWS - start
        return remote(
            ig_far.at[r, :, pl.ds(start, size)], ig_ref.at[0, :, own_columns(r, start, size)],
            y_s, yi_r, pair,
        )

    def make_ig(r):
        transposed = (((1,), (1,)), ((), ()))

        @pl.loop(0, ROWS // 128)
        def _(i):
            start = pl.multiple_of(i * 128, 128)
            product = lax.dot_general(
                cot[...], wb[r, pl.ds(start, 128), :], transposed, preferred_element_type=F32
            ).astype(BF16)
            ig_ref[0, :, own_columns(r, start, 128)] = product[:TOK]
            ig_far[r, :, pl.ds(start, 128)] = product[TOK:]

        ig_sent(r).start()
        if r != 4:
            ig_ref[0, :, pair_columns(r, 0, PURE)] = lax.dot_general(
                cot[:TOK, :], wb[r, ROWS:, :], transposed, preferred_element_type=F32
            ).astype(BF16)

    def pass_on(r, i):
        for d in (UP, DOWN):
            if i == 0:
                gather(d, r, first[d]).wait_recv()
            else:
                arrived(ag_r.at[d, r, 1], HALF + PURE)
            if r + 1 < 3:
                for c in (first[d],) if i == 0 else (1 - first[d], 2):
                    gather(d, r + 1, c).start()
            else:
                for c in (0, 1) if i == 0 else (2,):
                    fourth_start(d, c)

    pl.semaphore_wait(
        barrier, 2 + count(z > 0) + count(z == Z - 1) + count(q != ROOT) + count(high_root)
    )
    y_w.start()
    y_c.start()
    pl.when(z > 0)(lambda: greet(above, down))
    pl.when(z == Z - 1)(lambda: greet(below, up))

    def start_gather(d):
        gather(d, 0, first[d]).start()
        gather(d, 0, 1 - first[d]).start()

    pl.when(z > 0)(lambda: start_gather(DOWN))
    for s in (4, 3, 5, 2):
        y_x[s].start()
    pl.when(z < Z - 1)(lambda: pl.semaphore_wait(above, 1))
    start_gather(UP)
    pl.when(q != ROOT)(lambda: greet(here, root))
    for copy in local:
        copy.start()
    for s in (4, 3, 5, 2, 6, 1, 7, 0):
        own_x[s].start()

    @pl.when(z == 0)
    def _():
        pl.semaphore_wait(below, 1)
        start_gather(DOWN)

    @pl.when(high_root)
    def _():
        pl.semaphore_wait(here, PLANE - 1)
        greet(here, far)

    @pl.when(low_root)
    def _():
        pl.semaphore_wait(here, PLANE)
        for j in range(1, ISLANDS):
            greet(all_in, (lax.rem(isl + j, ISLANDS), fs))

    @pl.when(isl != ROOT)
    def _():
        pl.semaphore_wait(all_in, 1)

    for copy in c_1:
        copy.start()
    y_w.wait_recv()
    for d in (UP, DOWN):
        gather(d, 0, 2).start()
    pass_on(0, 0)
    loaded(lm, 256 + 512 + 64 + 1024 + 1024)
    loaded(lx, 8 * 256)
    arrived(c1_r, 7 * 64)

    def plane_sum(part):
        total = pg_own[part, :].astype(F32)
        for j in range(1, PLANE):
            total = total + c_in[j - 1, part, :].astype(F32)
        c_out[part, :] = total.astype(BF16)

    by_rows(0, PIECE, 16, plane_sum)
    c_2.start()
    for s in (6, 1, 7, 0):
        y_x[s].start()
    y_c.wait_recv()
    make_ig(0)
    pass_on(0, 1)
    make_term(4)
    make_ig(1)
    make_ig(7)
    pass_on(1, 0)
    make_term(3)
    make_term(5)
    pass_on(1, 1)
    make_ig(2)
    make_ig(6)
    make_term(2)
    pass_on(2, 0)
    c_2.wait_recv()
    avg[own_piece, :] = (c_out[...].astype(F32) + c_far[...].astype(F32)) * (1.0 / 16)
    for copy in c_3:
        copy.start()
    make_term(6)
    pass_on(2, 1)
    for d in (UP, DOWN):
        send_sum(d, 4, half_of[d][0], False)
    for d in (UP, DOWN):
        send_sum(d, 3, half_of[d][1], False)
    make_ig(3)
    make_ig(5)
    make_term(1)
    arrived(ag4_r, ROWS)
    make_ig(4)
    make_term(7)
    for d in (UP, DOWN):
        send_sum(d, 3, half_of[d][0], True)
    make_term(0)
    for h in (1, 0):
        for d in (UP, DOWN):
            send_sum(d, 2, half_of[d][h], True)

    arrived(c3_r, 7 * 128)

    def update(part):
        average = avg[part, :]
        momentum = outer_beta * omb[part, :] + average
        nm_ref[part, :] = momentum
        np_ref[part, :] = opb[part, :] - outer_rate * (average + outer_beta * momentum)

    by_rows(0, ROWS, 16, update)

    for h in (1, 0):
        for d in (UP, DOWN):
            send_sum(d, 1, half_of[d][h], True)

    sent(c1_s, 7 * 64)
    sent(c3_s, 7 * 128)
    sent(ag_s, 2 * 3 * (ROWS + PURE))
    def fourth_sent(size):
        part = wb.at[0, rows(0, size)]
        remote(part, part, ag4_s, ag4_s, pair).wait_send()

    less = (z == 0) | (z == Z - 1)
    more = (z == 1) | (z == Z - 2)
    pl.when(less)(lambda: fourth_sent(ROWS - SIDE))
    pl.when(more)(lambda: fourth_sent(ROWS + SIDE))
    pl.when(jnp.logical_not(less | more))(lambda: fourth_sent(ROWS))

    for last in (False, True):
        for d in (UP, DOWN):
            h = half_of[d][0 if last else 1]
            reduce_copy(d, 1, h).wait_recv()

            def add(part):
                arrived = rs_in[d, 0, part, :].astype(F32)
                if last:
                    wg_ref[0, part, :] = (wg_ref[0, part, :] + arrived) * (1.0 / 4096)
                else:
                    wg_ref[0, part, :] = term[0, part, :] + arrived

            by_rows(h * HALF, HALF, 32, add)

    sent(rs_s, 2 * 7 * HALF)
    sent(y_s, PURE + TOK + 8 * TOK + PIECE + 7 * (TOK * 3 // 4) + TOK)
    arrived(yi_r, 7 * (TOK * 3 // 4) + TOK)


def finish_kernel(a, b, c, d, a_out, b_out, c_out, d_out, sems):
    copies = [pltpu.make_async_copy(x, y, sems.at[n]) for n, (x, y) in enumerate(
        [(a, a_out), (b, b_out), (c, c_out), (d, d_out)])]
    for copy in copies:
        copy.start()
    for copy in copies:
        copy.wait()


def finish(*arrays):
    return pl.pallas_call(
        finish_kernel,
        name="finish",
        out_shape=tuple(jax.ShapeDtypeStruct(x.shape, x.dtype) for x in arrays),
        in_specs=[pl.BlockSpec(memory_space=pltpu.VMEM)] * 4,
        out_specs=(pl.BlockSpec(memory_space=pltpu.HBM),) * 4,
        scratch_shapes=[pltpu.SemaphoreType.DMA((4,))],
        compiler_params=pltpu.CompilerParams(vmem_limit_bytes=2**20),
    )(*[pltpu.with_memory_space_constraint(x, pltpu.VMEM) for x in arrays])


def body(inputs, cotangent, key_weight, pseudo_grads, outer_params, outer_momentum):
    dma = pltpu.SemaphoreType.DMA
    vmem = pltpu.VMEM
    anywhere = pl.BlockSpec(memory_space=pltpu.HBM)
    return finish(*pl.pallas_call(
        kernel,
        name="key_backward",
        out_shape=(
            vmem((1, TOK, 2 * Z * ROWS), BF16),
            vmem((1, ROWS, KW), F32),
            vmem((ROWS, KW), F32),
            vmem((ROWS, KW), F32),
        ),
        in_specs=[anywhere] * 6,
        out_specs=(pl.BlockSpec(memory_space=vmem),) * 4,
        scratch_shapes=[
            vmem((2 * TOK, KW), BF16),
            vmem((Z, 2 * TOK, ROWS), BF16),
            vmem((Z, ROWS + PURE, KW), BF16),
            vmem((Z, ROWS, KW), F32),
            vmem((2, 4, ROWS, KW), BF16),
            vmem((2, 4, ROWS, KW), BF16),
            vmem((Z, TOK, ROWS), BF16),
            vmem((PIECE, KW), BF16),
            vmem((PLANE - 1, PIECE, KW), BF16),
            vmem((PIECE, KW), BF16),
            vmem((PIECE, KW), BF16),
            vmem((ROWS, KW), F32),
            vmem((ROWS, KW), F32),
            vmem((ROWS, KW), F32),
            dma, dma, dma, dma, dma, dma,
            dma((2, 3, 2)), dma, dma((2, 7)), dma((Z,)), dma, dma,
            dma, dma, dma, dma, dma, dma,
        ]
        + [pltpu.SemaphoreType.REGULAR] * 4,
        compiler_params=pltpu.CompilerParams(
            collective_id=0, has_side_effects=True, vmem_limit_bytes=54 * 2**20
        ),
        cost_estimate=pl.CostEstimate(
            flops=4 * TOK * 2 * Z * ROWS * KW, bytes_accessed=24 * 2**20, transcendentals=0
        ),
    )(inputs, cotangent, key_weight, pseudo_grads, outer_params, outer_momentum))


def solution(mesh):
    return jax.shard_map(
        body,
        mesh=mesh,
        in_specs=(
            P("island", "fsdp", None),
            P("island", "fsdp", None),
            P("island", "fsdp", None),
            P("island", "fsdp", None),
            P("fsdp", None),
            P("fsdp", None),
        ),
        out_specs=(
            P("island", "fsdp", None),
            P("island", "fsdp", None),
            P("fsdp", None),
            P("fsdp", None),
        ),
        check_vma=False,
    )
```
